128 devices in a mesh: prow: 16 (over x, y), pcol: 8 (over z, core).
Axes of the slice: x: 4, y: 4, z: 4, core: 2. Of those that a mesh axis runs over, the one named last changes fastest.
Arguments:
- trailing: float32 [16384, 16384], P('prow', 'pcol'), may hold values from -6 to 6
- factors: float32 [64, 16384], P(None, ('prow', 'pcol')), may hold values from -1 to 1
- pivots: int32 [64], replicated, may hold values from 0 to 16383, as said below
Outputs:
- updated: float32 [16384, 16384], P('prow', 'pcol')
The draws below stay inside these ranges and needn't reach their ends.
Inputs may be any that keep to these rules, and one draw needn't show every extreme that they name: Entry j of pivots is j or larger.
All inputs are finite; a program needn't handle non-finite values.
Results may differ from the reference program's by a relative error of at most 0.000064.
Values sent between devices are 32-bit elements; how exact they have to be, the bound alone decides.
No kernel may reach another device: no remote copies, remote signals or barrier semaphores. Data moves between devices by JAX's collectives and lax.ppermute only.
A program may use at most 64 MiB of HBM per device.

```python
import jax
import jax.numpy as jnp
from jax import lax

NB = 64
ROWS_DEV = 1024
ROWS = 16384
COLS = 16384
N_PROW = 16


def draw_factors(key, part):
    key = jax.random.fold_in(key, 11)
    values = jax.random.uniform(key, (NB, ROWS), jnp.float32, -1.0, 1.0)
    column = lax.broadcasted_iota(jnp.int32, (NB, ROWS), 1)
    return jnp.where(column < NB, 0.125 * values, values)


def draw_pivots(key, part):
    key = jax.random.fold_in(key, 23)
    first_key, second_key = jax.random.split(key)
    places = jnp.arange(NB, dtype=jnp.int32)
    raw_values = jax.random.randint(first_key, (NB,), 0, 1 << 30, dtype=jnp.int32)
    chosen_rows = places + raw_values % (ROWS - places)
    marked = jax.random.randint(second_key, (), 0, NB, dtype=jnp.int32)
    return jnp.where(places == marked, ROWS - 1, chosen_rows).astype(jnp.int32)


def block_scale(own_key, dims, pieces, low, top_value):
    level = 1.0
    for position, blocks in pieces:
        heights = jax.random.uniform(jax.random.fold_in(jax.random.fold_in(own_key, 6), position), (blocks,), jnp.float32, low / len(pieces), top_value / len(pieces))
        level = level * jnp.repeat(jnp.exp(heights), dims[position] // blocks).reshape((-1,) + (1,) * (len(dims) - 1 - position))
    return level


def normal_values(rng, extent, spread, limit, shards=(), kind=jnp.bfloat16):
    drawn = jax.random.normal(rng, extent, jnp.float32) * spread
    if len(shards) > 0:
        drawn = block_scale(rng, extent, shards, -0.22, 0.18) * drawn
    return jnp.clip(drawn, min=-limit, max=limit).astype(kind)


def setup_inputs(seed: int = 0) -> dict:
    seeds = jax.random.split(jax.random.key(seed), 4)
    trailing = normal_values(seeds[0], (ROWS, COLS), 1.0, 6.0, ((0, 16), (1, 8)), jnp.float32)
    factors = draw_factors(jax.random.fold_in(seeds[3], 71), 0)
    pivots = draw_pivots(jax.random.fold_in(seeds[3], 71), 0)
    return {"trailing": trailing, "factors": factors, "pivots": pivots}


def to_matrix(stored):
    cols = stored.shape[1]
    blocks = stored.reshape(N_PROW, ROWS_DEV // NB, NB, cols)
    return jnp.transpose(blocks, (1, 0, 2, 3)).reshape(ROWS, cols)

def from_matrix(ordered):
    cols = ordered.shape[1]
    blocks = ordered.reshape(ROWS_DEV // NB, N_PROW, NB, cols)
    return jnp.transpose(blocks, (1, 0, 2, 3)).reshape(ROWS, cols)

def reference(trailing, factors, pivots):
    ordered = to_matrix(trailing)
    panel_rows = to_matrix(jnp.transpose(factors))

    def apply_swap(j, order_rows):
        k = pivots[j]
        a = order_rows[j]
        b = order_rows[k]
        return order_rows.at[j].set(b).at[k].set(a)
    order_rows = lax.fori_loop(0, NB, apply_swap, jnp.arange(ROWS, dtype=jnp.int32))
    swapped = jnp.take(ordered, order_rows, axis=0)
    unit_lower = panel_rows[:NB]
    upper_rows = jax.scipy.linalg.solve_triangular(unit_lower, swapped[:NB], lower=True, unit_diagonal=True)
    trailing_rows = swapped[NB:] - jnp.dot(panel_rows[NB:].astype(jnp.float32), upper_rows.astype(jnp.float32), precision=lax.Precision.HIGHEST, preferred_element_type=jnp.float32)
    return from_matrix(jnp.concatenate([upper_rows, trailing_rows], axis=0))
```

```python
import functools

import jax
import jax.numpy as jnp
from jax import lax
from jax.experimental import pallas as pl
from jax.experimental.pallas import tpu as pltpu
from jax.sharding import PartitionSpec as P

LANES = 128
NB = 64
N_PROW = 16
N_PCOL = 8
ROWS = 16384
EXTRA = 64
DISPLACED = 64
LOWER = 32
SEND_ROWS = NB + EXTRA
BACK_ROWS = NB + DISPLACED + LOWER
F32 = jnp.float32
BF16 = jnp.bfloat16


def holder_of(row):
    return (row // NB) % N_PROW


def local_of(row):
    return row // (NB * N_PROW) * NB + row % NB


def pick_kernel(pivots, trailing, sent, top_from, moved, own, order, count, sem):
    me = lax.axis_index("prow")

    def touch(j, carry):
        order[pivots[j]] = pivots[j]
        return carry

    def touch_top(j, carry):
        order[j] = j
        return carry

    def swap(j, carry):
        k = pivots[j]
        a = order[j]
        b = order[k]
        order[j] = b
        order[k] = a
        return carry

    def row_copy(row, slot, piece):
        return pltpu.make_async_copy(
            trailing.at[pl.ds(row, 1), pl.ds(piece * LANES, LANES)],
            sent.at[piece, pl.ds(slot, 1), :],
            sem,
        )

    def top_copy(piece):
        return pltpu.make_async_copy(
            trailing.at[pl.ds(0, NB), pl.ds(piece * LANES, LANES)],
            sent.at[piece, pl.ds(0, NB), :],
            sem,
        )

    @pl.when(me == 0)
    def _():
        for piece in range(N_PROW):
            top_copy(piece).start()

    lax.fori_loop(0, NB, touch, 0)
    lax.fori_loop(0, NB, touch_top, 0)
    lax.fori_loop(0, NB, swap, 0)

    def send(j, extras):
        row = order[j]
        holder = holder_of(row)
        is_extra = jnp.logical_and(holder == 0, row >= NB)
        slot = jnp.where(holder == 0, jnp.where(row < NB, row, NB + extras), j)
        top_from[j] = holder * SEND_ROWS + slot

        @pl.when(jnp.logical_and(holder == me, row >= NB))
        def _():
            for piece in range(N_PROW):
                row_copy(local_of(row), slot, piece).start()

        return extras + jnp.where(is_extra, 1, 0)

    lax.fori_loop(0, NB, send, 0)

    def clear(q, carry):
        count[q] = 0
        return carry

    lax.fori_loop(0, N_PROW, clear, 0)

    def place(j, carry):
        row = pivots[j]
        outside = row >= NB
        q = jnp.where(outside, holder_of(row), 0)
        slot = count[q]
        count[q] = slot + jnp.where(outside, 1, 0)
        moved[2 * j] = jnp.where(outside, q * BACK_ROWS + NB + slot, -1)
        moved[2 * j + 1] = jnp.where(outside, order[row], 0)

        @pl.when(jnp.logical_and(outside, q == me))
        def _():
            own[1 + slot] = local_of(row)

        return carry

    lax.fori_loop(0, NB, place, 0)
    own[0] = count[me]

    @pl.when(me == 0)
    def _():
        for piece in range(N_PROW):
            top_copy(piece).wait()

    def finish(j, carry):
        row = order[j]

        @pl.when(jnp.logical_and(holder_of(row) == me, row >= NB))
        def _():
            for piece in range(N_PROW):
                row_copy(0, 0, piece).wait()

        return carry

    lax.fori_loop(0, NB, finish, 0)


def pick(pivots, trailing):
    return pl.pallas_call(
        pick_kernel,
        out_shape=(
            jax.ShapeDtypeStruct((N_PROW, SEND_ROWS, LANES), F32),
            jax.ShapeDtypeStruct((NB,), jnp.int32),
            jax.ShapeDtypeStruct((2 * NB,), jnp.int32),
            jax.ShapeDtypeStruct((2 * NB,), jnp.int32),
        ),
        in_specs=[pl.BlockSpec(memory_space=pltpu.SMEM), pl.BlockSpec(memory_space=pl.ANY)],
        out_specs=(
            pl.BlockSpec(memory_space=pltpu.VMEM),
            pl.BlockSpec(memory_space=pltpu.SMEM),
            pl.BlockSpec(memory_space=pltpu.SMEM),
            pl.BlockSpec(memory_space=pltpu.SMEM),
        ),
        scratch_shapes=[
            pltpu.SMEM((ROWS,), jnp.int32),
            pltpu.SMEM((N_PROW,), jnp.int32),
            pltpu.SemaphoreType.DMA,
        ],
        compiler_params=pltpu.CompilerParams(vmem_limit_bytes=32 * 2**20),
    )(pivots, trailing)


def spread_kernel(top_from, moved, got, diagonal, back):
    def gather(j, carry):
        back[pl.ds(j, 1), :] = got[pl.ds(top_from[j], 1), :]
        return carry

    lax.fori_loop(0, NB, gather, 0)
    half = NB // 2
    for q in range(N_PROW):
        base = q * BACK_ROWS
        if q > 0:
            back[base : base + NB, :] = back[0:NB, :]
        low = base + NB + DISPLACED
        back[low : low + half, 0:NB] = diagonal[0:half, 0:NB]
        back[low : low + half, NB:LANES] = diagonal[half:NB, 0:NB]

    def displace(j, carry):
        target = moved[2 * j]

        @pl.when(target >= 0)
        def _():
            back[pl.ds(target, 1), :] = got[pl.ds(moved[2 * j + 1], 1), :]

        return carry

    lax.fori_loop(0, NB, displace, 0)


def spread(top_from, moved, got, diagonal):
    return pl.pallas_call(
        spread_kernel,
        out_shape=jax.ShapeDtypeStruct((N_PROW * BACK_ROWS, LANES), F32),
        in_specs=[
            pl.BlockSpec(memory_space=pltpu.SMEM),
            pl.BlockSpec(memory_space=pltpu.SMEM),
            pl.BlockSpec(memory_space=pltpu.VMEM),
            pl.BlockSpec(memory_space=pltpu.VMEM),
        ],
        out_specs=pl.BlockSpec(memory_space=pltpu.VMEM),
        compiler_params=pltpu.CompilerParams(vmem_limit_bytes=32 * 2**20),
    )(top_from, moved, got, diagonal)


def halves(x):
    high = x.astype(BF16)
    return high, (x - high.astype(F32)).astype(BF16)


def thirds(x):
    high = x.astype(BF16)
    rest = x - high.astype(F32)
    mid = rest.astype(BF16)
    return high, mid, (rest - mid.astype(F32)).astype(BF16)


CHUNK = 512
N_CHUNK = 4


def update_kernel(
    own, given, panel, trailing, updated, block, multipliers, columns, arrive, leave
):
    me = lax.axis_index("prow")

    def load(k):
        cols = pl.ds(k * CHUNK, CHUNK)
        return pltpu.make_async_copy(trailing.at[:, cols], block.at[:, cols], arrive.at[k])

    def store(k):
        cols = pl.ds(k * CHUNK, CHUNK)
        return pltpu.make_async_copy(block.at[:, cols], updated.at[:, cols], leave.at[k])

    for k in range(N_CHUNK):
        load(k).start()

    for c in range(N_PCOL):
        high, low = halves(panel[c * NB : (c + 1) * NB, :].T)
        rows = slice(c * LANES, (c + 1) * LANES)
        multipliers[rows, :] = jnp.concatenate([high, low, high, low], axis=1)

    packed = given[NB + DISPLACED : BACK_ROWS, :]
    stacked = jnp.concatenate([packed[:, 0:NB], packed[:, NB:LANES]], axis=0)
    lower = stacked.T
    row_id = lax.broadcasted_iota(jnp.int32, (NB, NB), 0)
    col_id = lax.broadcasted_iota(jnp.int32, (NB, NB), 1)
    lower = jnp.where(col_id < row_id, lower, 0.0)
    for j in range(NB):
        columns[j] = jnp.broadcast_to(lower[:, j : j + 1], (NB, LANES))

    row_id = lax.broadcasted_iota(jnp.int32, (8, LANES), 0)
    col_id = lax.broadcasted_iota(jnp.int32, (8, LANES), 1)
    inverse = [jnp.where(col_id == row_id + 8 * b, 1.0, 0.0).astype(F32) for b in range(8)]
    for j in range(NB):
        b, s = j // 8, j % 8
        row = jnp.broadcast_to(inverse[b][s : s + 1, :], (8, LANES))
        for i in range(b, 8):
            inverse[i] = inverse[i] - columns[j, 8 * i : 8 * i + 8, :] * row
    inv_high, inv_mid, inv_low = thirds(jnp.concatenate(inverse, axis=0)[:, 0:NB])
    left = jnp.concatenate([inv_high, inv_mid, inv_low, inv_high, inv_mid, inv_high], axis=1)

    n_own = own[0]
    for k in range(N_CHUNK):
        cols = slice(k * CHUNK, (k + 1) * CHUNK)
        pieces = range(k * CHUNK // LANES, (k + 1) * CHUNK // LANES)
        swapped = jnp.concatenate(
            [given[p * BACK_ROWS : p * BACK_ROWS + NB, :] for p in pieces], axis=1
        )
        high, mid, low = thirds(swapped)
        right = jnp.concatenate([high, high, high, mid, mid, low], axis=0)
        upper = jnp.dot(left, right, preferred_element_type=F32)
        up_high, up_low = halves(upper)
        factor = jnp.concatenate([up_high, up_high, up_low, up_low], axis=0)
        load(k).wait()

        def displace(slot, carry):
            row = own[1 + slot]
            group = pl.ds(pl.multiple_of(row // 8 * 8, 8), 8)
            for p in pieces:
                source = given[pl.ds(p * BACK_ROWS + NB + slot, 1), :]
                part = slice(p * LANES, (p + 1) * LANES)
                block[group, part] = jnp.where(row_id == row % 8, source, block[group, part])
            return carry

        lax.fori_loop(0, n_own, displace, 0)
        product = jnp.dot(multipliers[...], factor, preferred_element_type=F32)
        block[:, cols] = block[:, cols] - product

        @pl.when(me == 0)
        def _():
            block[0:NB, cols] = upper

        store(k).start()
    for k in range(N_CHUNK):
        store(k).wait()


def update(own, given, panel, trailing):
    rows, cols = trailing.shape
    return pl.pallas_call(
        update_kernel,
        out_shape=jax.ShapeDtypeStruct((rows, cols), F32),
        in_specs=[
            pl.BlockSpec(memory_space=pltpu.SMEM),
            pl.BlockSpec(memory_space=pltpu.VMEM),
            pl.BlockSpec(memory_space=pltpu.VMEM),
            pl.BlockSpec(memory_space=pl.ANY),
        ],
        out_specs=pl.BlockSpec(memory_space=pl.ANY),
        scratch_shapes=[
            pltpu.VMEM((rows, cols), F32),
            pltpu.VMEM((rows, 4 * NB), BF16),
            pltpu.VMEM((NB, NB, LANES), F32),
            pltpu.SemaphoreType.DMA((N_CHUNK,)),
            pltpu.SemaphoreType.DMA((N_CHUNK,)),
        ],
        compiler_params=pltpu.CompilerParams(vmem_limit_bytes=48 * 2**20),
    )(own, given, panel, trailing)


def body(trailing, factors, pivots):
    sent, top_from, moved, own = pick(pivots, trailing)
    copies = jnp.broadcast_to(factors[None], (N_PCOL, NB, LANES))
    panel = lax.all_to_all(copies, "pcol", 0, 0)
    got = lax.all_to_all(sent, "prow", 0, 0)
    back = spread(top_from, moved, got.reshape(N_PROW * SEND_ROWS, LANES), panel[0])
    given = lax.all_to_all(back.reshape(N_PROW, BACK_ROWS, LANES), "prow", 0, 0)
    return update(
        own,
        given.reshape(N_PROW * BACK_ROWS, LANES),
        panel.reshape(N_PCOL * NB, LANES),
        trailing,
    )


def solution(mesh):
    return jax.shard_map(
        body,
        mesh=mesh,
        in_specs=(P("prow", "pcol"), P(None, ("prow", "pcol")), P()),
        out_specs=P("prow", "pcol"),
        check_vma=False,
    )
```

```python
import functools

import jax
import jax.numpy as jnp
from jax import lax
from jax.experimental import pallas as pl
from jax.experimental.pallas import tpu as pltpu
from jax.sharding import PartitionSpec as P

LANES = 128
NB = 64
N_PROW = 16
N_PCOL = 8
ROWS = 16384
FEW = 16
LOWER = 16
F32 = jnp.float32
BF16 = jnp.bfloat16


def holder_of(row):
    return (row >> 6) & (N_PROW - 1)


def local_of(row):
    return ((row >> 10) << 6) | (row & (NB - 1))


def swap_chain(pivots, order, visit):
    for j in range(NB):
        order[pivots[j]] = pivots[j]
    for j in range(NB):
        order[j] = j
    for j in range(NB):
        k = pivots[j]
        row = order[k]
        order[k] = order[j]
        visit(j, row)


def swap_chain(pivots, order, visit):
    for j in range(NB):
        order[pivots[j]] = pivots[j]
    for j in range(NB):
        order[j] = j
    for j in range(NB):
        k = pivots[j]
        row = order[k]
        order[k] = order[j]
        visit(j, row)


def pick_kernel(pivots, trailing, sent, more, state, order, count, sem, top_sem):
    me = lax.axis_index("prow")

    def row_copy(row, slot, piece, target):
        return pltpu.make_async_copy(
            trailing.at[pl.ds(row, 1), pl.ds(piece * LANES, LANES)],
            target.at[piece, pl.ds(slot, 1), :],
            sem,
        )

    def top_copy(piece):
        return pltpu.make_async_copy(
            trailing.at[pl.ds(0, NB), pl.ds(piece * LANES, LANES)],
            sent.at[piece, pl.ds(0, NB), :],
            top_sem.at[piece],
        )

    @pl.when(me == 0)
    def _():
        for piece in range(N_PROW):
            top_copy(piece).start()

    count[N_PROW] = 0
    count[N_PROW + 1] = 0

    def visit(j, row):
        holder = holder_of(row)
        extra = count[N_PROW + 1]
        is_extra = jnp.logical_and(holder == 0, row >= NB)
        count[N_PROW + 1] = extra + jnp.where(is_extra, 1, 0)

        @pl.when(jnp.logical_and(holder == me, row >= NB))
        def _():
            count[N_PROW] = count[N_PROW] + 1
            slot = jnp.where(me == 0, NB + extra, j)
            local = local_of(row)

            @pl.when(slot < NB + FEW)
            def _():
                for piece in range(N_PROW):
                    row_copy(local, slot, piece, sent).start()

            @pl.when(slot >= NB + FEW)
            def _():
                for piece in range(N_PROW):
                    row_copy(local, slot - (NB + FEW), piece, more).start()

    swap_chain(pivots, order, visit)
    for q in range(N_PROW):
        count[q] = 0
    for j in range(NB):
        row = pivots[j]
        q = holder_of(row)
        count[q] = count[q] + jnp.where(row >= NB, 1, 0)
    most = count[N_PROW + 1]
    for q in range(N_PROW):
        most = jnp.maximum(most, count[q])
    state[0] = me
    state[1] = jnp.where(most > FEW, 1, 0)

    @pl.when(me == 0)
    def _():
        for piece in range(N_PROW):
            top_copy(piece).wait()

    def finish(i, carry):
        for piece in range(N_PROW):
            row_copy(0, 0, piece, sent).wait()
        return carry

    lax.fori_loop(0, count[N_PROW], finish, 0)


def pick(pivots, trailing):
    return pl.pallas_call(
        pick_kernel,
        out_shape=(
            jax.ShapeDtypeStruct((N_PROW, NB + FEW, LANES), F32),
            jax.ShapeDtypeStruct((N_PROW, NB - FEW, LANES), F32),
            jax.ShapeDtypeStruct((2,), jnp.int32),
        ),
        in_specs=[
            pl.BlockSpec(memory_space=pltpu.SMEM),
            pl.BlockSpec(memory_space=pltpu.HBM),
        ],
        out_specs=(
            pl.BlockSpec(memory_space=pltpu.VMEM),
            pl.BlockSpec(memory_space=pltpu.VMEM),
            pl.BlockSpec(memory_space=pltpu.SMEM),
        ),
        scratch_shapes=[
            pltpu.SMEM((ROWS,), jnp.int32),
            pltpu.SMEM((N_PROW + 2,), jnp.int32),
            pltpu.SemaphoreType.DMA,
            pltpu.SemaphoreType.DMA((N_PROW,)),
        ],
        compiler_params=pltpu.CompilerParams(vmem_limit_bytes=58 * 2**20),
    )(pivots, trailing)


TOP_FROM = 0
MOVED = NB
OWN = 3 * NB
TABLE = 5 * NB


def route_kernel(room, pivots, state, mine, other, table, pair, order, count):
    send_rows, back_rows = NB + room, NB + room + LOWER
    me = state[0]
    pair[0:NB, :] = mine[...]
    pair[NB : 2 * NB, :] = other[...]
    count[N_PROW] = 0

    def visit(j, row):
        holder = holder_of(row)
        extra = count[N_PROW]
        count[N_PROW] = extra + jnp.where(jnp.logical_and(holder == 0, row >= NB), 1, 0)
        slot = jnp.where(holder == 0, jnp.where(row < NB, row, NB + extra), j)
        table[TOP_FROM + j] = holder * send_rows + slot

    swap_chain(pivots, order, visit)
    for q in range(N_PROW):
        count[q] = 0
    for j in range(NB):
        row = pivots[j]
        outside = row >= NB
        q = jnp.where(outside, holder_of(row), 0)
        slot = count[q]
        count[q] = slot + jnp.where(outside, 1, 0)
        table[MOVED + 2 * j] = jnp.where(outside, q * back_rows + NB + slot, -1)
        table[MOVED + 2 * j + 1] = jnp.where(outside, order[row], 0)

        @pl.when(jnp.logical_and(outside, q == me))
        def _():
            table[OWN + 1 + slot] = local_of(row)

    table[OWN] = count[me]


def route(room, pivots, state, mine, other):
    smem = pl.BlockSpec(memory_space=pltpu.SMEM)
    vmem = pl.BlockSpec(memory_space=pltpu.VMEM)
    return pl.pallas_call(
        functools.partial(route_kernel, room),
        out_shape=(
            jax.ShapeDtypeStruct((TABLE,), jnp.int32),
            jax.ShapeDtypeStruct((2 * NB, LANES), F32),
        ),
        in_specs=[smem, smem, vmem, vmem],
        out_specs=(smem, vmem),
        scratch_shapes=[
            pltpu.SMEM((ROWS,), jnp.int32),
            pltpu.SMEM((N_PROW + 1,), jnp.int32),
        ],
    )(pivots, state, mine, other)


HALF = NB // 2


def fold(diagonal):
    row_id = lax.broadcasted_iota(jnp.int32, (HALF, HALF), 0)
    col_id = lax.broadcasted_iota(jnp.int32, (HALF, HALF), 1)
    first = diagonal[0:HALF, 0:HALF]
    last = diagonal[HALF:NB, HALF:NB]
    mixed = jnp.where(col_id > row_id, first, last.T)
    both = jnp.concatenate([mixed, diagonal[0:HALF, HALF:NB]], axis=1)
    return jnp.concatenate([both[0:LOWER], both[LOWER:HALF]], axis=1)


def unfold(packed):
    row_id = lax.broadcasted_iota(jnp.int32, (HALF, HALF), 0)
    col_id = lax.broadcasted_iota(jnp.int32, (HALF, HALF), 1)
    both = jnp.concatenate([packed[:, 0:NB], packed[:, NB:LANES]], axis=0)
    mixed = both[:, 0:HALF]
    zero = jnp.zeros((HALF, HALF), F32)
    first = jnp.where(col_id < row_id, mixed.T, zero)
    last = jnp.where(col_id < row_id, mixed, zero)
    top = jnp.concatenate([first, zero], axis=1)
    return jnp.concatenate([top, jnp.concatenate([both[:, HALF:NB].T, last], axis=1)], axis=0)


def spread_kernel(room, table, got, here, below, above, across, back, diagonal):
    back_rows = NB + room + LOWER
    c = lax.axis_index("pcol")
    z, core = c // 2, c % 2
    for place, pair in enumerate((here, below, across, above)):

        @pl.when(z == place)
        def _():
            start = pl.multiple_of(core * NB, NB)
            diagonal[...] = pair[pl.ds(start, NB), :]

    for j in range(NB):
        back[j : j + 1, :] = got[pl.ds(table[TOP_FROM + j], 1), :]
    packed = fold(diagonal[:, 0:NB])
    for q in range(N_PROW):
        base = q * back_rows
        if q > 0:
            back[base : base + NB, :] = back[0:NB, :]
        low = base + NB + room
        back[low : low + LOWER, :] = packed

    for j in range(NB):
        target = table[MOVED + 2 * j]

        @pl.when(target >= 0)
        def _():
            back[pl.ds(target, 1), :] = got[pl.ds(table[MOVED + 2 * j + 1], 1), :]


def spread(room, table, got, pairs):
    vmem = pl.BlockSpec(memory_space=pltpu.VMEM)
    back_rows = NB + room + LOWER
    return pl.pallas_call(
        functools.partial(spread_kernel, room),
        out_shape=jax.ShapeDtypeStruct((N_PROW * back_rows, LANES), F32),
        in_specs=[pl.BlockSpec(memory_space=pltpu.SMEM)] + [vmem] * 5,
        out_specs=vmem,
        scratch_shapes=[pltpu.VMEM((NB, LANES), F32)],
        compiler_params=pltpu.CompilerParams(vmem_limit_bytes=32 * 2**20),
    )(table, got, *pairs)


def halves(x):
    high = x.astype(BF16)
    return high, (x - high.astype(F32)).astype(BF16)


def thirds(x):
    high = x.astype(BF16)
    rest = x - high.astype(F32)
    mid = rest.astype(BF16)
    return high, mid, (rest - mid.astype(F32)).astype(BF16)


CHUNK = 512
N_CHUNK = 4


def update_kernel(
    room,
    table,
    given,
    here,
    below,
    above,
    across,
    trailing,
    updated,
    block,
    multipliers,
    columns,
    arrive,
    leave,
):
    back_rows = NB + room + LOWER
    me = lax.axis_index("prow")
    c = lax.axis_index("pcol")
    z, core = c // 2, c % 2

    def load(k):
        cols = pl.ds(k * CHUNK, CHUNK)
        return pltpu.make_async_copy(trailing.at[:, cols], block.at[:, cols], arrive.at[k])

    def store(k):
        cols = pl.ds(k * CHUNK, CHUNK)
        return pltpu.make_async_copy(block.at[:, cols], updated.at[:, cols], leave.at[k])

    for k in range(N_CHUNK):
        load(k).start()

    for step, pair in ((0, here), (3, below), (1, above), (2, across)):
        for side in range(2):
            high, low = halves(pair[side * NB : (side + 1) * NB, :].T)
            place = ((z + step) % 4) * 2 + (core + side) % 2
            start = pl.multiple_of(place * LANES, LANES)
            multipliers[pl.ds(start, LANES), :] = jnp.concatenate([high, low, high, low], axis=1)

    lower = unfold(given[NB + room : back_rows, :])
    for j in range(NB):
        columns[j] = jnp.broadcast_to(lower[:, j : j + 1], (NB, LANES))

    row_id = lax.broadcasted_iota(jnp.int32, (8, LANES), 0)
    col_id = lax.broadcasted_iota(jnp.int32, (8, LANES), 1)
    inverse = [jnp.where(col_id == row_id + 8 * b, 1.0, 0.0).astype(F32) for b in range(8)]
    for j in range(NB):
        b, s = j // 8, j % 8
        row = jnp.broadcast_to(inverse[b][s : s + 1, :], (8, LANES))
        for i in range(b, 8):
            inverse[i] = inverse[i] - columns[j, 8 * i : 8 * i + 8, :] * row
    inv_high, inv_mid, inv_low = thirds(jnp.concatenate(inverse, axis=0)[:, 0:NB])
    left = jnp.concatenate([inv_high, inv_mid, inv_low, inv_high, inv_mid, inv_high], axis=1)

    n_own = table[OWN]
    for k in range(N_CHUNK):
        cols = slice(k * CHUNK, (k + 1) * CHUNK)
        pieces = range(k * CHUNK // LANES, (k + 1) * CHUNK // LANES)
        swapped = jnp.concatenate(
            [given[p * back_rows : p * back_rows + NB, :] for p in pieces], axis=1
        )
        high, mid, low = thirds(swapped)
        right = jnp.concatenate([high, high, high, mid, mid, low], axis=0)
        upper = jnp.dot(left, right, preferred_element_type=F32)
        up_high, up_low = halves(upper)
        factor = jnp.concatenate([up_high, up_high, up_low, up_low], axis=0)
        load(k).wait()

        def displace(slot, carry):
            row = table[OWN + 1 + slot]
            group = pl.ds(pl.multiple_of(row // 8 * 8, 8), 8)
            for p in pieces:
                source = given[pl.ds(p * back_rows + NB + slot, 1), :]
                part = slice(p * LANES, (p + 1) * LANES)
                block[group, part] = jnp.where(row_id == row % 8, source, block[group, part])
            return carry

        lax.fori_loop(0, n_own, displace, 0)
        product = jnp.dot(multipliers[...], factor, preferred_element_type=F32)
        block[:, cols] = block[:, cols] - product

        @pl.when(me == 0)
        def _():
            block[0:NB, cols] = upper

        store(k).start()
    for k in range(N_CHUNK):
        store(k).wait()


def update(room, table, given, pairs, trailing):
    rows, cols = trailing.shape
    vmem = pl.BlockSpec(memory_space=pltpu.VMEM)
    return pl.pallas_call(
        functools.partial(update_kernel, room),
        out_shape=jax.ShapeDtypeStruct((rows, cols), F32),
        in_specs=[pl.BlockSpec(memory_space=pltpu.SMEM)]
        + [vmem] * 5
        + [pl.BlockSpec(memory_space=pltpu.HBM)],
        out_specs=pl.BlockSpec(memory_space=pltpu.HBM),
        scratch_shapes=[
            pltpu.VMEM((rows, cols), F32),
            pltpu.VMEM((rows, 4 * NB), BF16),
            pltpu.VMEM((NB, NB, LANES), F32),
            pltpu.SemaphoreType.DMA((N_CHUNK,)),
            pltpu.SemaphoreType.DMA((N_CHUNK,)),
        ],
        compiler_params=pltpu.CompilerParams(vmem_limit_bytes=58 * 2**20),
    )(table, given, *pairs, trailing)


def ring(step):
    return [(c, (c // 2 + step) % 4 * 2 + c % 2) for c in range(N_PCOL)]


def rest(room, trailing, factors, partner, pivots, sent, state):
    got = lax.all_to_all(sent, "prow", 0, 0)
    table, pair = route(room, pivots, state, factors, partner)
    below = lax.ppermute(pair, "pcol", ring(1))
    above = lax.ppermute(pair, "pcol", ring(3))
    across = lax.ppermute(pair, "pcol", ring(2))
    pairs = (pair, below, above, across)
    back = spread(room, table, got.reshape(-1, LANES), pairs)
    given = lax.all_to_all(back.reshape(N_PROW, -1, LANES), "prow", 0, 0)
    return update(room, table, given.reshape(-1, LANES), pairs, trailing)


def body(trailing, factors, pivots):
    partner = lax.ppermute(factors, "pcol", [(c, c ^ 1) for c in range(N_PCOL)])
    sent, more, state = pick(pivots, trailing)

    def few(sent, more):
        return rest(FEW, trailing, factors, partner, pivots, sent, state)

    def many(sent, more):
        every = jnp.concatenate([sent, more], axis=1)
        return rest(NB, trailing, factors, partner, pivots, every, state)

    return lax.cond(state[1] == 0, few, many, sent, more)


def solution(mesh):
    return jax.shard_map(
        body,
        mesh=mesh,
        in_specs=(P("prow", "pcol"), P(None, ("prow", "pcol")), P()),
        out_specs=P("prow", "pcol"),
        check_vma=False,
    )
```

```python
import functools

import jax
import jax.numpy as jnp
from jax import lax
from jax.experimental import pallas as pl
from jax.experimental.pallas import tpu as pltpu
from jax.sharding import PartitionSpec as P

LANES = 128
NB = 64
N_PROW = 16
N_PCOL = 8
ROWS = 16384
FEW = 16
LOWER = 16
F32 = jnp.float32
BF16 = jnp.bfloat16


def holder_of(row):
    return (row >> 6) & (N_PROW - 1)


def local_of(row):
    return ((row >> 10) << 6) | (row & (NB - 1))


def swap_chain(pivots, order, visit):
    for j in range(NB):
        order[pivots[j]] = pivots[j]
    for j in range(NB):
        order[j] = j
    for j in range(NB):
        k = pivots[j]
        row = order[k]
        order[k] = order[j]
        visit(j, row)


def pick_kernel(room, pivots, trailing, sent, order, count, mine, sem, top_sem):
    me = lax.axis_index("prow")

    def row_copy(row, slot, piece):
        return pltpu.make_async_copy(
            trailing.at[pl.ds(row, 1), pl.ds(piece * LANES, LANES)],
            sent.at[piece, pl.ds(slot, 1), :],
            sem,
        )

    def top_copy(piece):
        return pltpu.make_async_copy(
            trailing.at[pl.ds(0, NB), pl.ds(piece * LANES, LANES)],
            sent.at[piece, pl.ds(0, NB), :],
            top_sem.at[piece],
        )

    @pl.when(me == 0)
    def _():
        for piece in range(N_PROW):
            top_copy(piece).start()

    count[0] = 0

    def visit(j, row):
        place = count[0]
        mine[2 * place] = local_of(row)
        mine[2 * place + 1] = jnp.where(me == 0, NB + place, j)
        wanted = jnp.logical_and(holder_of(row) == me, row >= NB)
        count[0] = place + jnp.where(wanted, 1, 0)

    swap_chain(pivots, order, visit)
    n_mine = jnp.where(me == 0, jnp.minimum(count[0], room), count[0])

    def send(i, carry):
        for piece in range(N_PROW):
            row_copy(mine[2 * i], mine[2 * i + 1], piece).start()
        return carry

    lax.fori_loop(0, n_mine, send, 0)

    @pl.when(me == 0)
    def _():
        for piece in range(N_PROW):
            top_copy(piece).wait()

    def finish(i, carry):
        for piece in range(N_PROW):
            row_copy(0, 0, piece).wait()
        return carry

    lax.fori_loop(0, n_mine, finish, 0)


SMEM = pl.BlockSpec(memory_space=pltpu.SMEM)
VMEM = pl.BlockSpec(memory_space=pltpu.VMEM)
HBM = pl.BlockSpec(memory_space=pltpu.HBM)
ANY = pl.BlockSpec(memory_space=pl.ANY)


def pick(room, pivots, trailing):
    return pl.pallas_call(
        functools.partial(pick_kernel, room),
        out_shape=jax.ShapeDtypeStruct((N_PROW, NB + room, LANES), F32),
        in_specs=[SMEM, HBM],
        out_specs=VMEM,
        scratch_shapes=[
            pltpu.SMEM((ROWS,), jnp.int32),
            pltpu.SMEM((1,), jnp.int32),
            pltpu.SMEM((2 * NB + 2,), jnp.int32),
            pltpu.SemaphoreType.DMA,
            pltpu.SemaphoreType.DMA((N_PROW,)),
        ],
        compiler_params=pltpu.CompilerParams(vmem_limit_bytes=58 * 2**20),
    )(pivots, trailing)


def join_kernel(mine, other, pair):
    pair[0:NB, :] = mine[...]
    pair[NB : 2 * NB, :] = other[...]


def join(mine, other):
    return pl.pallas_call(
        join_kernel,
        out_shape=jax.ShapeDtypeStruct((2 * NB, LANES), F32),
        in_specs=[VMEM, VMEM],
        out_specs=VMEM,
        compiler_params=pltpu.CompilerParams(vmem_limit_bytes=8 * 2**20),
    )(mine, other)


MOVED = NB
ROUTES = 3 * NB
OWN = 2 * NB


def route_kernel(room, pivots, routes, owned, over, table, own, order, count, sems):
    send_rows, back_rows = NB + room, NB + room + LOWER
    me = lax.axis_index("prow")
    for q in range(N_PROW + 1):
        count[q] = 0

    def visit(j, row):
        holder = holder_of(row)
        extra = count[N_PROW]
        count[N_PROW] = extra + jnp.where(jnp.logical_and(holder == 0, row >= NB), 1, 0)
        spare = NB + jnp.minimum(extra, room - 1)
        slot = jnp.where(holder == 0, jnp.where(row < NB, row, spare), j)
        table[0, j] = holder * send_rows + slot

    swap_chain(pivots, order, visit)

    for j in range(NB):
        row = pivots[j]
        outside = row >= NB
        q = jnp.where(outside, holder_of(row), 0)
        slot = count[q]
        count[q] = slot + jnp.where(outside, 1, 0)
        fits = jnp.logical_and(outside, slot < room)
        table[0, MOVED + 2 * j] = jnp.where(fits, q * back_rows + NB + slot, 0)
        table[0, MOVED + 2 * j + 1] = jnp.where(outside, order[row], 0)
        here = jnp.logical_and(outside, q == me)
        own[0, jnp.where(here, 1 + slot, OWN - 1)] = local_of(row)

    own[0, 0] = jnp.minimum(count[me], room)
    most = count[N_PROW]
    for q in range(N_PROW):
        most = jnp.maximum(most, count[q])
    over[0] = jnp.where(most > room, 1, 0)
    first = pltpu.make_async_copy(table, routes, sems.at[0])
    second = pltpu.make_async_copy(own, owned, sems.at[1])
    first.start()
    second.start()
    first.wait()
    second.wait()


def route(room, pivots):
    return pl.pallas_call(
        functools.partial(route_kernel, room),
        out_shape=(
            jax.ShapeDtypeStruct((1, ROUTES), jnp.int32),
            jax.ShapeDtypeStruct((1, OWN), jnp.int32),
            jax.ShapeDtypeStruct((1,), jnp.int32),
        ),
        in_specs=[SMEM],
        out_specs=(VMEM, VMEM, SMEM),
        scratch_shapes=[
            pltpu.SMEM((1, ROUTES), jnp.int32),
            pltpu.SMEM((1, OWN), jnp.int32),
            pltpu.SMEM((ROWS,), jnp.int32),
            pltpu.SMEM((N_PROW + 1,), jnp.int32),
            pltpu.SemaphoreType.DMA((2,)),
        ],
        compiler_params=pltpu.CompilerParams(vmem_limit_bytes=8 * 2**20),
    )(pivots)


HALF = NB // 2


def fold(diagonal):
    row_id = lax.broadcasted_iota(jnp.int32, (HALF, HALF), 0)
    col_id = lax.broadcasted_iota(jnp.int32, (HALF, HALF), 1)
    first = diagonal[0:HALF, 0:HALF]
    last = diagonal[HALF:NB, HALF:NB]
    mixed = jnp.where(col_id > row_id, first, last.T)
    both = jnp.concatenate([mixed, diagonal[0:HALF, HALF:NB]], axis=1)
    return jnp.concatenate([both[0:LOWER], both[LOWER:HALF]], axis=1)


def unfold(packed):
    row_id = lax.broadcasted_iota(jnp.int32, (HALF, HALF), 0)
    col_id = lax.broadcasted_iota(jnp.int32, (HALF, HALF), 1)
    both = jnp.concatenate([packed[:, 0:NB], packed[:, NB:LANES]], axis=0)
    mixed = both[:, 0:HALF]
    zero = jnp.zeros((HALF, HALF), F32)
    first = jnp.where(col_id < row_id, mixed.T, zero)
    last = jnp.where(col_id < row_id, mixed, zero)
    top = jnp.concatenate([first, zero], axis=1)
    return jnp.concatenate([top, jnp.concatenate([both[:, HALF:NB].T, last], axis=1)], axis=0)


def spread_kernel(
    room, routes, got, mine, other, below, above, across, back, table, diagonal, sem
):
    copy = pltpu.make_async_copy(routes, table, sem)
    copy.start()
    back_rows = NB + room + LOWER
    c = lax.axis_index("pcol")
    z, core = c // 2, c % 2
    start = pl.multiple_of(core * NB, NB)

    @pl.when(c == 0)
    def _():
        diagonal[...] = mine[...]

    @pl.when(c == 1)
    def _():
        diagonal[...] = other[...]

    for place, pair in ((1, below), (2, across), (3, above)):

        @pl.when(z == place)
        def _():
            diagonal[...] = pair[pl.ds(start, NB), :]

    packed = fold(diagonal[:, 0:NB])
    for q in range(N_PROW):
        low = q * back_rows + NB + room
        back[low : low + LOWER, :] = packed
    copy.wait()

    for j in range(NB):
        source = got[pl.ds(table[0, MOVED + 2 * j + 1], 1), :]
        back[pl.ds(table[0, MOVED + 2 * j], 1), :] = source
    for j in range(NB):
        back[j : j + 1, :] = got[pl.ds(table[0, j], 1), :]
    for q in range(1, N_PROW):
        base = q * back_rows
        back[base : base + NB, :] = back[0:NB, :]


def spread(room, routes, got, panels):
    back_rows = NB + room + LOWER
    return pl.pallas_call(
        functools.partial(spread_kernel, room),
        out_shape=jax.ShapeDtypeStruct((N_PROW * back_rows, LANES), F32),
        in_specs=[ANY] + [VMEM] * 6,
        out_specs=VMEM,
        scratch_shapes=[
            pltpu.SMEM((1, ROUTES), jnp.int32),
            pltpu.VMEM((NB, LANES), F32),
            pltpu.SemaphoreType.DMA,
        ],
        compiler_params=pltpu.CompilerParams(vmem_limit_bytes=16 * 2**20),
    )(routes, got, *panels)


def halves(x):
    high = x.astype(BF16)
    return high, (x - high.astype(F32)).astype(BF16)


def thirds(x):
    high = x.astype(BF16)
    rest = x - high.astype(F32)
    mid = rest.astype(BF16)
    return high, mid, (rest - mid.astype(F32)).astype(BF16)


HEAD = 256
WIDEST = 512
CHUNKS = ((0, HEAD), (256, 512), (768, 512), (1280, 512), (1792, 256))


def prepare_kernel(back, trailing, mine, other, below, above, across, head, multipliers, sem):
    del back
    c = lax.axis_index("pcol")
    z, core = c // 2, c % 2
    load = pltpu.make_async_copy(trailing.at[:, pl.ds(0, HEAD)], head, sem)
    load.start()

    def place(step, side, values):
        high, low = halves(values.T)
        start = (((z + step) & 3) * 2 + ((core + side) & 1)) * LANES
        rows = pl.ds(pl.multiple_of(start, LANES), LANES)
        multipliers[rows, :] = jnp.concatenate([high, low, high, low], axis=1)

    place(0, 0, mine[...])
    place(0, 1, other[...])
    for step, pair in ((3, below), (1, above), (2, across)):
        place(step, 0, pair[0:NB, :])
        place(step, 1, pair[NB : 2 * NB, :])
    load.wait()


def prepare(back, trailing, panels):
    rows, cols = trailing.shape
    return pl.pallas_call(
        prepare_kernel,
        out_shape=(
            jax.ShapeDtypeStruct((rows, HEAD), F32),
            jax.ShapeDtypeStruct((rows, 4 * NB), BF16),
        ),
        in_specs=[ANY, HBM] + [VMEM] * 5,
        out_specs=(VMEM, VMEM),
        scratch_shapes=[pltpu.SemaphoreType.DMA],
        compiler_params=pltpu.CompilerParams(vmem_limit_bytes=24 * 2**20),
        cost_estimate=pl.CostEstimate(flops=0, bytes_accessed=4 * rows * cols, transcendentals=0),
    )(back, trailing, *panels)


def update_kernel(
    room, owned, given, multipliers, head, trailing, updated, block, products, own, columns, arrive, leave, sem
):
    back_rows = NB + room + LOWER
    me = lax.axis_index("prow")

    def load(k):
        cols = pl.ds(*CHUNKS[k])
        return pltpu.make_async_copy(trailing.at[:, cols], block.at[:, cols], arrive.at[k])

    def store(k):
        cols = pl.ds(*CHUNKS[k])
        return pltpu.make_async_copy(block.at[:, cols], updated.at[:, cols], leave.at[k])

    copy = pltpu.make_async_copy(owned, own, sem)
    copy.start()
    for k in range(1, len(CHUNKS)):
        load(k).start()

    lower = unfold(given[NB + room : back_rows, :])
    for j in range(NB):
        columns[j] = jnp.broadcast_to(lower[:, j : j + 1], (NB, LANES))

    row_id = lax.broadcasted_iota(jnp.int32, (8, LANES), 0)
    col_id = lax.broadcasted_iota(jnp.int32, (8, LANES), 1)
    inverse = [jnp.where(col_id == row_id + 8 * b, 1.0, 0.0).astype(F32) for b in range(8)]
    for j in range(NB):
        b, s = j // 8, j % 8
        row = jnp.broadcast_to(inverse[b][s : s + 1, :], (8, LANES))
        for i in range(b, 8):
            inverse[i] = inverse[i] - columns[j, 8 * i : 8 * i + 8, :] * row
    inv_high, inv_mid, inv_low = thirds(jnp.concatenate(inverse, axis=0)[:, 0:NB])
    left = jnp.concatenate([inv_high, inv_mid, inv_low, inv_high, inv_mid, inv_high], axis=1)

    copy.wait()
    n_own = own[0, 0]
    for k, (start, width) in enumerate(CHUNKS):
        cols = slice(start, start + width)
        pieces = range(start // LANES, (start + width) // LANES)
        swapped = jnp.concatenate(
            [given[p * back_rows : p * back_rows + NB, :] for p in pieces], axis=1
        )
        high, mid, low = thirds(swapped)
        right = jnp.concatenate([high, high, high, mid, mid, low], axis=0)
        upper = jnp.dot(left, right, preferred_element_type=F32)
        up_high, up_low = halves(upper)
        factor = jnp.concatenate([up_high, up_high, up_low, up_low], axis=0)

        part = slice(0, width)
        products[:, part] = jnp.dot(multipliers[...], factor, preferred_element_type=F32)
        if k == 0:
            block[:, cols] = head[...] - products[:, part]
        else:
            load(k).wait()
            block[:, cols] = block[:, cols] - products[:, part]

        def displace(slot, carry):
            row = own[0, 1 + slot]
            group = pl.ds(pl.multiple_of(row // 8 * 8, 8), 8)
            for n, p in enumerate(pieces):
                moved = given[pl.ds(p * back_rows + NB + slot, 1), :]
                part = slice(p * LANES, (p + 1) * LANES)
                change = moved - products[group, n * LANES : (n + 1) * LANES]
                block[group, part] = jnp.where(row_id == row % 8, change, block[group, part])
            return carry

        lax.fori_loop(0, n_own, displace, 0)

        @pl.when(me == 0)
        def _():
            block[0:NB, cols] = upper

        store(k).start()
    for k in range(len(CHUNKS)):
        store(k).wait()


def update(room, owned, given, multipliers, head, trailing):
    rows, cols = trailing.shape
    return pl.pallas_call(
        functools.partial(update_kernel, room),
        out_shape=jax.ShapeDtypeStruct((rows, cols), F32),
        in_specs=[VMEM] * 4 + [HBM],
        out_specs=HBM,
        scratch_shapes=[
            pltpu.VMEM((rows, cols), F32),
            pltpu.VMEM((rows, WIDEST), F32),
            pltpu.SMEM((1, OWN), jnp.int32),
            pltpu.VMEM((NB, NB, LANES), F32),
            pltpu.SemaphoreType.DMA((len(CHUNKS),)),
            pltpu.SemaphoreType.DMA((len(CHUNKS),)),
            pltpu.SemaphoreType.DMA,
        ],
        compiler_params=pltpu.CompilerParams(vmem_limit_bytes=48 * 2**20),
    )(owned, given, multipliers, head, trailing)


def ring(step):
    return [(c, (c // 2 + step) % 4 * 2 + c % 2) for c in range(N_PCOL)]


def step(room, trailing, factors, partner, pivots):
    sent = pick(room, pivots, trailing)
    got = lax.all_to_all(sent, "prow", 0, 0)
    pair = join(factors, partner)
    below = lax.ppermute(pair, "pcol", ring(1))
    above = lax.ppermute(pair, "pcol", ring(3))
    across = lax.ppermute(pair, "pcol", ring(2))
    routes, owned, over = route(room, pivots)
    panels = (factors, partner, below, above, across)
    back = spread(room, routes, got.reshape(-1, LANES), panels)
    given = lax.all_to_all(back.reshape(N_PROW, -1, LANES), "prow", 0, 0)
    head, multipliers = prepare(back, trailing, panels)
    updated = update(room, owned, given.reshape(-1, LANES), multipliers, head, trailing)
    return updated, over


def body(trailing, factors, pivots):
    partner = lax.ppermute(factors, "pcol", [(c, c ^ 1) for c in range(N_PCOL)])
    updated, over = step(FEW, trailing, factors, partner, pivots)

    def again(updated):
        return step(NB, trailing, factors, partner, pivots)[0]

    return lax.cond(over[0] == 0, lambda updated: updated, again, updated)


def solution(mesh):
    return jax.shard_map(
        body,
        mesh=mesh,
        in_specs=(P("prow", "pcol"), P(None, ("prow", "pcol")), P()),
        out_specs=P("prow", "pcol"),
        check_vma=False,
    )
```

```python
import jax
import jax.numpy as jnp
from jax import lax
from jax.experimental import pallas as pl
from jax.experimental.pallas import tpu as pltpu
from jax.sharding import PartitionSpec as P

LANES = 128
NB = 64
N_PROW = 16
N_PCOL = 8
ROWS = 16384
LOWER = 16
BACK = NB + LOWER
F32 = jnp.float32
BF16 = jnp.bfloat16


def holder_of(row):
    return (row >> 6) & (N_PROW - 1)


def local_of(row):
    return ((row >> 10) << 6) | (row & (NB - 1))


def swap_chain(pivots, order, visit):
    for j in range(NB):
        order[pivots[j]] = pivots[j]
    for j in range(NB):
        order[j] = j
    for j in range(NB):
        k = pivots[j]
        row = order[k]
        order[k] = order[j]
        visit(j, row)


def pick_kernel(pivots, trailing, sent, order, count, rows, slots, sem, top_sem):
    me = lax.axis_index("prow")

    def row_copy(row, slot, piece):
        return pltpu.make_async_copy(
            trailing.at[pl.ds(row, 1), pl.ds(piece * LANES, LANES)],
            sent.at[piece, pl.ds(slot, 1), :],
            sem,
        )

    def top_copy(piece):
        return pltpu.make_async_copy(
            trailing.at[pl.ds(0, NB), pl.ds(piece * LANES, LANES)],
            sent.at[piece, pl.ds(0, NB), :],
            top_sem.at[piece],
        )

    @pl.when(me == 0)
    def _():
        for piece in range(N_PROW):
            top_copy(piece).start()

    count[0] = 0

    def visit(j, row):
        place = count[0]
        rows[place] = row
        slots[place] = j
        wanted = jnp.logical_and(holder_of(row) == me, row >= NB)
        count[0] = place + jnp.where(wanted, 1, 0)

    swap_chain(pivots, order, visit)
    n_mine = count[0]

    @pl.when(me == 0)
    def _():
        for piece in range(N_PROW):
            top_copy(piece).wait()

    def send(i, carry):
        row = rows[i]
        slot = jnp.where(me == 0, order[row], slots[i])
        for piece in range(N_PROW):
            row_copy(local_of(row), slot, piece).start()
        return carry

    lax.fori_loop(0, n_mine, send, 0)

    def finish(i, carry):
        for piece in range(N_PROW):
            row_copy(0, 0, piece).wait()
        return carry

    lax.fori_loop(0, n_mine, finish, 0)


SMEM = pl.BlockSpec(memory_space=pltpu.SMEM)
VMEM = pl.BlockSpec(memory_space=pltpu.VMEM)
HBM = pl.BlockSpec(memory_space=pltpu.HBM)
ANY = pl.BlockSpec(memory_space=pl.ANY)


def pick(pivots, trailing):
    return pl.pallas_call(
        pick_kernel,
        out_shape=jax.ShapeDtypeStruct((N_PROW, NB, LANES), F32),
        in_specs=[SMEM, HBM],
        out_specs=VMEM,
        scratch_shapes=[
            pltpu.SMEM((ROWS,), jnp.int32),
            pltpu.SMEM((1,), jnp.int32),
            pltpu.SMEM((NB + 1,), jnp.int32),
            pltpu.SMEM((NB + 1,), jnp.int32),
            pltpu.SemaphoreType.DMA,
            pltpu.SemaphoreType.DMA((N_PROW,)),
        ],
        compiler_params=pltpu.CompilerParams(vmem_limit_bytes=58 * 2**20),
    )(pivots, trailing)


def join_kernel(mine, other, pair):
    pair[0:NB, :] = mine[...]
    pair[NB : 2 * NB, :] = other[...]


def join(mine, other):
    return pl.pallas_call(
        join_kernel,
        out_shape=jax.ShapeDtypeStruct((2 * NB, LANES), F32),
        in_specs=[VMEM, VMEM],
        out_specs=VMEM,
        compiler_params=pltpu.CompilerParams(vmem_limit_bytes=8 * 2**20),
    )(mine, other)


TARGET = NB
SOURCE = 2 * NB
ROUTES = 3 * NB
OWN = 2 * NB


def route_kernel(pivots, routes, owned, table, own, order, rows, count, sems):
    me = lax.axis_index("prow")

    def visit(j, row):
        rows[j] = row

    swap_chain(pivots, order, visit)
    count[0] = 0
    for j in range(NB):
        row = rows[j]
        holder = holder_of(row)
        outside = row >= NB
        displacer = jnp.where(outside, order[row], row)
        place = holder * NB + jnp.where(holder == 0, displacer, j)
        away = holder > 0
        table[0, j] = place
        table[0, TARGET + j] = holder * BACK + j
        table[0, SOURCE + j] = jnp.where(away, displacer, place)
        slot = count[0]
        own[0, 1 + slot] = local_of(row) * NB + jnp.where(away, j, displacer)
        count[0] = slot + jnp.where(jnp.logical_and(outside, holder == me), 1, 0)
    own[0, 0] = count[0]
    first = pltpu.make_async_copy(table, routes, sems.at[0])
    second = pltpu.make_async_copy(own, owned, sems.at[1])
    first.start()
    second.start()
    first.wait()
    second.wait()


def route(pivots):
    return pl.pallas_call(
        route_kernel,
        out_shape=(
            jax.ShapeDtypeStruct((1, ROUTES), jnp.int32),
            jax.ShapeDtypeStruct((1, OWN), jnp.int32),
        ),
        in_specs=[SMEM],
        out_specs=(VMEM, VMEM),
        scratch_shapes=[
            pltpu.SMEM((1, ROUTES), jnp.int32),
            pltpu.SMEM((1, OWN), jnp.int32),
            pltpu.SMEM((ROWS,), jnp.int32),
            pltpu.SMEM((NB,), jnp.int32),
            pltpu.SMEM((1,), jnp.int32),
            pltpu.SemaphoreType.DMA((2,)),
        ],
        compiler_params=pltpu.CompilerParams(vmem_limit_bytes=8 * 2**20),
    )(pivots)


HALF = NB // 2


def fold(diagonal):
    row_id = lax.broadcasted_iota(jnp.int32, (HALF, HALF), 0)
    col_id = lax.broadcasted_iota(jnp.int32, (HALF, HALF), 1)
    first = diagonal[0:HALF, 0:HALF]
    last = diagonal[HALF:NB, HALF:NB]
    mixed = jnp.where(col_id > row_id, first, last.T)
    both = jnp.concatenate([mixed, diagonal[0:HALF, HALF:NB]], axis=1)
    return jnp.concatenate([both[0:LOWER], both[LOWER:HALF]], axis=1)


def unfold(packed):
    row_id = lax.broadcasted_iota(jnp.int32, (HALF, HALF), 0)
    col_id = lax.broadcasted_iota(jnp.int32, (HALF, HALF), 1)
    both = jnp.concatenate([packed[:, 0:NB], packed[:, NB:LANES]], axis=0)
    mixed = both[:, 0:HALF]
    zero = jnp.zeros((HALF, HALF), F32)
    first = jnp.where(col_id < row_id, mixed.T, zero)
    last = jnp.where(col_id < row_id, mixed, zero)
    top = jnp.concatenate([first, zero], axis=1)
    return jnp.concatenate([top, jnp.concatenate([both[:, HALF:NB].T, last], axis=1)], axis=0)


def spread_kernel(routes, got, *refs):
    panels, (back, table, diagonal, sem) = refs[:5], refs[5:]
    copy = pltpu.make_async_copy(routes, table, sem)
    copy.start()
    c = lax.axis_index("pcol")
    start = pl.multiple_of(c % 2 * NB, NB)
    for side in range(2):

        @pl.when(c == side)
        def _():
            diagonal[...] = panels[side][...]

    for step, pair in enumerate(panels[2:], 1):

        @pl.when(c // 2 == 4 - step)
        def _():
            diagonal[...] = pair[pl.ds(start, NB), :]

    packed = fold(diagonal[:, 0:NB])
    for q in range(N_PROW):
        low = q * BACK + NB
        back[low : low + LOWER, :] = packed
    copy.wait()
    for j in range(NB):
        back[j : j + 1, :] = got[pl.ds(table[0, j], 1), :]
    for q in range(1, N_PROW):
        back[q * BACK : q * BACK + NB, :] = back[0:NB, :]
    for j in range(NB):
        source = got[pl.ds(table[0, SOURCE + j], 1), :]
        back[pl.ds(table[0, TARGET + j], 1), :] = source


def spread(routes, got, panels):
    return pl.pallas_call(
        spread_kernel,
        out_shape=jax.ShapeDtypeStruct((N_PROW * BACK, LANES), F32),
        in_specs=[ANY] + [VMEM] * 6,
        out_specs=VMEM,
        scratch_shapes=[
            pltpu.SMEM((1, ROUTES), jnp.int32),
            pltpu.VMEM((NB, LANES), F32),
            pltpu.SemaphoreType.DMA,
        ],
        compiler_params=pltpu.CompilerParams(vmem_limit_bytes=16 * 2**20),
    )(routes, got, *panels)


def halves(x):
    high = x.astype(BF16)
    return high, (x - high.astype(F32)).astype(BF16)


def thirds(x):
    high = x.astype(BF16)
    rest = x - high.astype(F32)
    mid = rest.astype(BF16)
    return high, mid, (rest - mid.astype(F32)).astype(BF16)


CHUNKS = ((0, 256), (256, 512), (768, 512), (1280, 512), (1792, 256))


def update_kernel(
    owned,
    given,
    mine,
    other,
    *refs,
):
    pairs, refs = refs[:3], refs[3:]
    trailing, updated, block, multipliers, swapped, own, columns, arrive, leave, sem = refs
    me = lax.axis_index("prow")

    def load(k):
        cols = pl.ds(*CHUNKS[k])
        return pltpu.make_async_copy(trailing.at[:, cols], block.at[:, cols], arrive.at[k])

    def store(k):
        cols = pl.ds(*CHUNKS[k])
        return pltpu.make_async_copy(block.at[:, cols], updated.at[:, cols], leave.at[k])

    copy = pltpu.make_async_copy(owned, own, sem)
    copy.start()
    for k in range(len(CHUNKS)):
        load(k).start()

    c = lax.axis_index("pcol")
    z, core = c // 2, c % 2

    def place(step, side, values):
        high, low = halves(values.T)
        start = (((z + step) & 3) * 2 + ((core + side) & 1)) * LANES
        rows = pl.ds(pl.multiple_of(start, LANES), LANES)
        multipliers[rows, :] = jnp.concatenate([high, low, high, low], axis=1)

    for side, panel in enumerate((mine, other)):
        place(0, side, panel[...])
        for step, pair in enumerate(pairs, 1):
            place(step, side, pair[side * NB : (side + 1) * NB, :])

    lower = unfold(given[NB:BACK, :])
    for j in range(NB):
        columns[j] = jnp.broadcast_to(lower[:, j : j + 1], (NB, LANES))

    row_id = lax.broadcasted_iota(jnp.int32, (8, LANES), 0)
    col_id = lax.broadcasted_iota(jnp.int32, (8, LANES), 1)
    inverse = [jnp.where(col_id == row_id + 8 * b, 1.0, 0.0).astype(F32) for b in range(8)]
    for j in range(NB):
        b, s = j // 8, j % 8
        row = jnp.broadcast_to(inverse[b][s : s + 1, :], (8, LANES))
        for i in range(b, 8):
            inverse[i] = inverse[i] - columns[j, 8 * i : 8 * i + 8, :] * row
    inv_high, inv_mid, inv_low = thirds(jnp.concatenate(inverse, axis=0)[:, 0:NB])
    left = jnp.concatenate([inv_high, inv_mid, inv_low, inv_high, inv_mid, inv_high], axis=1)

    copy.wait()
    n_own = own[0, 0]
    n_away = jnp.where(me == 0, 0, n_own)
    n_here = n_own - n_away

    def group_of(row):
        return pl.ds(pl.multiple_of(row // 8 * 8, 8), 8), row_id == row % 8

    def row_of(ref, row, part):
        group, here = group_of(row)
        return jnp.sum(jnp.where(here, ref[group, part], 0.0), axis=0, keepdims=True)

    for k, (start, width) in enumerate(CHUNKS):
        cols = slice(start, start + width)
        pieces = range(start // LANES, (start + width) // LANES)
        parts = [slice(p * LANES, (p + 1) * LANES) for p in pieces]
        load(k).wait()
        for n, p in enumerate(pieces):
            swapped[n * NB : (n + 1) * NB, :] = given[p * BACK : p * BACK + NB, :]

        def fetch(i, carry):
            row, j = own[0, 1 + i] // NB, own[0, 1 + i] % NB
            for n, part in enumerate(parts):
                swapped[pl.ds(n * NB + j, 1), :] = row_of(block, row, part)
            return carry

        lax.fori_loop(0, n_away, fetch, 0)
        tops = jnp.concatenate([swapped[n * NB : (n + 1) * NB, :] for n in range(len(parts))], axis=1)
        high, mid, low = thirds(tops)
        right = jnp.concatenate([high, high, high, mid, mid, low], axis=0)
        upper = jnp.dot(left, right, preferred_element_type=F32)
        up_high, up_low = halves(upper)
        factor = jnp.concatenate([up_high, up_high, up_low, up_low], axis=0)
        product = jnp.dot(multipliers[...], factor, preferred_element_type=F32)

        def displace(i, carry):
            row, j = own[0, 1 + i] // NB, own[0, 1 + i] % NB
            group, here = group_of(row)
            for p, part in zip(pieces, parts):
                moved = given[pl.ds(p * BACK + j, 1), :]
                block[group, part] = jnp.where(here, moved, block[group, part])
            return carry

        def displace_here(i, carry):
            row, t = own[0, 1 + i] // NB, own[0, 1 + i] % NB
            group, here = group_of(row)
            for part in parts:
                moved = row_of(block, t, part)
                block[group, part] = jnp.where(here, moved, block[group, part])
            return carry

        lax.fori_loop(0, n_away, displace, 0)
        lax.fori_loop(0, n_here, displace_here, 0)
        block[:, cols] = block[:, cols] - product

        @pl.when(me == 0)
        def _():
            block[0:NB, cols] = upper

        store(k).start()
    for k in range(len(CHUNKS)):
        store(k).wait()


def update(owned, given, panels, trailing):
    rows, cols = trailing.shape
    return pl.pallas_call(
        update_kernel,
        out_shape=jax.ShapeDtypeStruct((rows, cols), F32),
        in_specs=[VMEM] * 7 + [HBM],
        out_specs=HBM,
        scratch_shapes=[
            pltpu.VMEM((rows, cols), F32),
            pltpu.VMEM((rows, 4 * NB), BF16),
            pltpu.VMEM((4 * NB, LANES), F32),
            pltpu.SMEM((1, OWN), jnp.int32),
            pltpu.VMEM((NB, NB, LANES), F32),
            pltpu.SemaphoreType.DMA((len(CHUNKS),)),
            pltpu.SemaphoreType.DMA((len(CHUNKS),)),
            pltpu.SemaphoreType.DMA,
        ],
        compiler_params=pltpu.CompilerParams(vmem_limit_bytes=48 * 2**20),
    )(owned, given, *panels, trailing)


def ring(step):
    return [(c, (c // 2 + step) % 4 * 2 + c % 2) for c in range(N_PCOL)]


def body(trailing, factors, pivots):
    partner = lax.ppermute(factors, "pcol", [(c, c ^ 1) for c in range(N_PCOL)])
    sent = pick(pivots, trailing)
    pair = join(factors, partner)
    got = lax.all_to_all(sent, "prow", 0, 0)
    panels = [factors, partner] + [lax.ppermute(pair, "pcol", ring(4 - turn)) for turn in (1, 2, 3)]
    routes, owned = route(pivots)
    back = spread(routes, got.reshape(N_PROW * NB, LANES), panels)
    given = lax.all_to_all(back.reshape(N_PROW, BACK, LANES), "prow", 0, 0)
    return update(owned, given.reshape(N_PROW * BACK, LANES), panels, trailing)


def solution(mesh):
    return jax.shard_map(
        body,
        mesh=mesh,
        in_specs=(P("prow", "pcol"), P(None, ("prow", "pcol")), P()),
        out_specs=P("prow", "pcol"),
        check_vma=False,
    )
```

```python
import jax
import jax.numpy as jnp
from jax import lax
from jax.experimental import pallas as pl
from jax.experimental.pallas import tpu as pltpu
from jax.sharding import PartitionSpec as P

LANES = 128
NB = 64
N_PROW = 16
N_PCOL = 8
ROWS = 16384
LOWER = 16
BACK = NB + LOWER
F32 = jnp.float32
BF16 = jnp.bfloat16


def holder_of(row):
    return (row >> 6) & (N_PROW - 1)


def local_of(row):
    return ((row >> 10) << 6) | (row & (NB - 1))


def swap_chain(pivots, order, visit):
    for j in range(NB):
        order[pivots[j]] = pivots[j]
    for j in range(NB):
        order[j] = j
    for j in range(NB):
        k = pivots[j]
        row = order[k]
        order[k] = order[j]
        visit(j, row)


def pick_kernel(pivots, trailing, sent, order, count, rows, slots, sem, top_sem):
    me = lax.axis_index("prow")

    def row_copy(row, slot, piece):
        return pltpu.make_async_copy(
            trailing.at[pl.ds(row, 1), pl.ds(piece * LANES, LANES)],
            sent.at[piece, pl.ds(slot, 1), :],
            sem,
        )

    def top_copy(piece):
        return pltpu.make_async_copy(
            trailing.at[pl.ds(0, NB), pl.ds(piece * LANES, LANES)],
            sent.at[piece, pl.ds(0, NB), :],
            top_sem.at[piece],
        )

    @pl.when(me == 0)
    def _():
        for piece in range(N_PROW):
            top_copy(piece).start()

    count[0] = 0

    def visit(j, row):
        place = count[0]
        rows[place] = row
        slots[place] = j
        wanted = jnp.logical_and(holder_of(row) == me, row >= NB)
        count[0] = place + jnp.where(wanted, 1, 0)

    swap_chain(pivots, order, visit)
    n_mine = count[0]

    @pl.when(me == 0)
    def _():
        for piece in range(N_PROW):
            top_copy(piece).wait()

    def send(i, carry):
        row = rows[i]
        slot = jnp.where(me == 0, order[row], slots[i])
        for piece in range(N_PROW):
            row_copy(local_of(row), slot, piece).start()
        return carry

    lax.fori_loop(0, n_mine, send, 0)

    def finish(i, carry):
        for piece in range(N_PROW):
            row_copy(0, 0, piece).wait()
        return carry

    lax.fori_loop(0, n_mine, finish, 0)


SMEM = pl.BlockSpec(memory_space=pltpu.SMEM)
VMEM = pl.BlockSpec(memory_space=pltpu.VMEM)
HBM = pl.BlockSpec(memory_space=pltpu.HBM)
ANY = pl.BlockSpec(memory_space=pl.ANY)


def pick(pivots, trailing):
    return pl.pallas_call(
        pick_kernel,
        out_shape=jax.ShapeDtypeStruct((N_PROW, NB, LANES), F32),
        in_specs=[SMEM, HBM],
        out_specs=VMEM,
        scratch_shapes=[
            pltpu.SMEM((ROWS,), jnp.int32),
            pltpu.SMEM((1,), jnp.int32),
            pltpu.SMEM((NB + 1,), jnp.int32),
            pltpu.SMEM((NB + 1,), jnp.int32),
            pltpu.SemaphoreType.DMA,
            pltpu.SemaphoreType.DMA((N_PROW,)),
        ],
        compiler_params=pltpu.CompilerParams(vmem_limit_bytes=58 * 2**20),
    )(pivots, trailing)


def join_kernel(mine, other, pair):
    pair[0:NB, :] = mine[...]
    pair[NB : 2 * NB, :] = other[...]


def join(mine, other):
    return pl.pallas_call(
        join_kernel,
        out_shape=jax.ShapeDtypeStruct((2 * NB, LANES), F32),
        in_specs=[VMEM, VMEM],
        out_specs=VMEM,
        compiler_params=pltpu.CompilerParams(vmem_limit_bytes=8 * 2**20),
    )(mine, other)


TARGET = NB
SOURCE = 2 * NB
ROUTES = 3 * NB
OWN = 2 * NB


def route_kernel(pivots, routes, owned, table, own, order, rows, count, sems):
    me = lax.axis_index("prow")

    def visit(j, row):
        rows[j] = row

    swap_chain(pivots, order, visit)
    count[0] = 0
    for j in range(NB):
        row = rows[j]
        holder = holder_of(row)
        outside = row >= NB
        displacer = jnp.where(outside, order[row], row)
        place = holder * NB + jnp.where(holder == 0, displacer, j)
        away = holder > 0
        table[0, j] = place
        table[0, TARGET + j] = holder * BACK + j
        table[0, SOURCE + j] = jnp.where(away, displacer, place)
        slot = count[0]
        own[0, 1 + slot] = local_of(row) * NB + jnp.where(away, j, displacer)
        count[0] = slot + jnp.where(jnp.logical_and(outside, holder == me), 1, 0)
    own[0, 0] = count[0]
    first = pltpu.make_async_copy(table, routes, sems.at[0])
    second = pltpu.make_async_copy(own, owned, sems.at[1])
    first.start()
    second.start()
    first.wait()
    second.wait()


def route(pivots):
    return pl.pallas_call(
        route_kernel,
        out_shape=(
            jax.ShapeDtypeStruct((1, ROUTES), jnp.int32),
            jax.ShapeDtypeStruct((1, OWN), jnp.int32),
        ),
        in_specs=[SMEM],
        out_specs=(VMEM, VMEM),
        scratch_shapes=[
            pltpu.SMEM((1, ROUTES), jnp.int32),
            pltpu.SMEM((1, OWN), jnp.int32),
            pltpu.SMEM((ROWS,), jnp.int32),
            pltpu.SMEM((NB,), jnp.int32),
            pltpu.SMEM((1,), jnp.int32),
            pltpu.SemaphoreType.DMA((2,)),
        ],
        compiler_params=pltpu.CompilerParams(vmem_limit_bytes=8 * 2**20),
    )(pivots)


HALF = NB // 2


def fold(diagonal):
    row_id = lax.broadcasted_iota(jnp.int32, (HALF, HALF), 0)
    col_id = lax.broadcasted_iota(jnp.int32, (HALF, HALF), 1)
    first = diagonal[0:HALF, 0:HALF]
    last = diagonal[HALF:NB, HALF:NB]
    mixed = jnp.where(col_id > row_id, first, last.T)
    both = jnp.concatenate([mixed, diagonal[0:HALF, HALF:NB]], axis=1)
    return jnp.concatenate([both[0:LOWER], both[LOWER:HALF]], axis=1)


def unfold(packed):
    row_id = lax.broadcasted_iota(jnp.int32, (HALF, HALF), 0)
    col_id = lax.broadcasted_iota(jnp.int32, (HALF, HALF), 1)
    both = jnp.concatenate([packed[:, 0:NB], packed[:, NB:LANES]], axis=0)
    mixed = both[:, 0:HALF]
    zero = jnp.zeros((HALF, HALF), F32)
    first = jnp.where(col_id < row_id, mixed.T, zero)
    last = jnp.where(col_id < row_id, mixed, zero)
    top = jnp.concatenate([first, zero], axis=1)
    return jnp.concatenate([top, jnp.concatenate([both[:, HALF:NB].T, last], axis=1)], axis=0)


def spread_kernel(routes, got, *refs):
    panels, (back, table, diagonal, sem) = refs[:5], refs[5:]
    copy = pltpu.make_async_copy(routes, table, sem)
    copy.start()
    c = lax.axis_index("pcol")
    start = pl.multiple_of(c % 2 * NB, NB)
    for side in range(2):

        @pl.when(c == side)
        def _():
            diagonal[...] = panels[side][...]

    for step, pair in enumerate(panels[2:], 1):

        @pl.when(c // 2 == 4 - step)
        def _():
            diagonal[...] = pair[pl.ds(start, NB), :]

    packed = fold(diagonal[:, 0:NB])
    for q in range(N_PROW):
        low = q * BACK + NB
        back[low : low + LOWER, :] = packed
    copy.wait()
    for j in range(NB):
        back[j : j + 1, :] = got[pl.ds(table[0, j], 1), :]
    for q in range(1, N_PROW):
        back[q * BACK : q * BACK + NB, :] = back[0:NB, :]
    for j in range(NB):
        source = got[pl.ds(table[0, SOURCE + j], 1), :]
        back[pl.ds(table[0, TARGET + j], 1), :] = source


def spread(routes, got, panels):
    return pl.pallas_call(
        spread_kernel,
        out_shape=jax.ShapeDtypeStruct((N_PROW * BACK, LANES), F32),
        in_specs=[ANY] + [VMEM] * 6,
        out_specs=VMEM,
        scratch_shapes=[
            pltpu.SMEM((1, ROUTES), jnp.int32),
            pltpu.VMEM((NB, LANES), F32),
            pltpu.SemaphoreType.DMA,
        ],
        compiler_params=pltpu.CompilerParams(vmem_limit_bytes=16 * 2**20),
    )(routes, got, *panels)


def halves(x):
    high = x.astype(BF16)
    return high, (x - high.astype(F32)).astype(BF16)


def thirds(x):
    high = x.astype(BF16)
    rest = x - high.astype(F32)
    mid = rest.astype(BF16)
    return high, mid, (rest - mid.astype(F32)).astype(BF16)


CHUNKS = ((0, 256), (256, 512), (768, 512), (1280, 512), (1792, 256))


def update_kernel(
    owned,
    given,
    mine,
    other,
    *refs,
):
    pairs, refs = refs[:3], refs[3:]
    trailing, updated, block, kept, chosen, tops_here, multipliers, own, columns = refs[:9]
    arrive, leave, sem, row_sem = refs[9:]
    me = lax.axis_index("prow")

    def load(k):
        cols = pl.ds(*CHUNKS[k])
        return pltpu.make_async_copy(trailing.at[:, cols], block.at[:, cols], arrive.at[k])

    def store(k):
        cols = pl.ds(*CHUNKS[k])
        return pltpu.make_async_copy(block.at[:, cols], updated.at[:, cols], leave.at[k])

    copy = pltpu.make_async_copy(owned, own, sem)
    copy.start()
    load(0).start()

    copy.wait()
    n_own = own[0, 0]
    n_away = jnp.where(me == 0, 0, n_own)
    n_here = n_own - n_away

    row_id = lax.broadcasted_iota(jnp.int32, (8, LANES), 0)

    def group_of(row):
        return pl.ds(pl.multiple_of(row // 8 * 8, 8), 8), row_id == row % 8

    def row_copy(i):
        row, j = own[0, 1 + i] // NB, own[0, 1 + i] % NB
        return pltpu.make_async_copy(
            trailing.at[pl.ds(row, 1), :], kept.at[pl.ds(j, 1), :], row_sem
        )

    def fetch(i, carry):
        row_copy(i).start()
        chosen[pl.ds(own[0, 1 + i] % NB, 1), :] = jnp.ones((1, LANES), F32)
        return carry

    def fetched(i, carry):
        row_copy(i).wait()
        return carry

    chosen[...] = jnp.zeros_like(chosen)
    lax.fori_loop(0, n_away, fetch, 0)
    for k in range(1, len(CHUNKS)):
        load(k).start()

    c = lax.axis_index("pcol")
    z, core = c // 2, c % 2

    def place(step, side, values):
        high, low = halves(values.T)
        start = (((z + step) & 3) * 2 + ((core + side) & 1)) * LANES
        rows = pl.ds(pl.multiple_of(start, LANES), LANES)
        multipliers[rows, :] = jnp.concatenate([high, low, high, low], axis=1)

    for side, panel in enumerate((mine, other)):
        place(0, side, panel[...])
        for step, pair in enumerate(pairs, 1):
            place(step, side, pair[side * NB : (side + 1) * NB, :])

    lower = unfold(given[NB:BACK, :])
    for j in range(NB):
        columns[j] = jnp.broadcast_to(lower[:, j : j + 1], (NB, LANES))

    row_id = lax.broadcasted_iota(jnp.int32, (8, LANES), 0)
    col_id = lax.broadcasted_iota(jnp.int32, (8, LANES), 1)
    inverse = [jnp.where(col_id == row_id + 8 * b, 1.0, 0.0).astype(F32) for b in range(8)]
    for j in range(NB):
        b, s = j // 8, j % 8
        row = jnp.broadcast_to(inverse[b][s : s + 1, :], (8, LANES))
        for i in range(b, 8):
            inverse[i] = inverse[i] - columns[j, 8 * i : 8 * i + 8, :] * row
    inv_high, inv_mid, inv_low = thirds(jnp.concatenate(inverse, axis=0)[:, 0:NB])
    left = jnp.concatenate([inv_high, inv_mid, inv_low, inv_high, inv_mid, inv_high], axis=1)

    lax.fori_loop(0, n_away, fetched, 0)
    for k, (start, width) in enumerate(CHUNKS):
        cols = slice(start, start + width)
        pieces = range(start // LANES, (start + width) // LANES)
        parts = [slice(p * LANES, (p + 1) * LANES) for p in pieces]
        load(k).wait()
        tops = jnp.concatenate(
            [
                jnp.where(chosen[...] > 0, kept[:, part], given[p * BACK : p * BACK + NB, :])
                for p, part in zip(pieces, parts)
            ],
            axis=1,
        )
        high, mid, low = thirds(tops)
        right = jnp.concatenate([high, high, high, mid, mid, low], axis=0)
        upper = jnp.dot(left, right, preferred_element_type=F32)
        up_high, up_low = halves(upper)
        factor = jnp.concatenate([up_high, up_high, up_low, up_low], axis=0)
        product = jnp.dot(multipliers[...], factor, preferred_element_type=F32)

        def displace(i, carry):
            row, j = own[0, 1 + i] // NB, own[0, 1 + i] % NB
            group, here = group_of(row)
            for p, part in zip(pieces, parts):
                moved = given[pl.ds(p * BACK + j, 1), :]
                block[group, part] = jnp.where(here, moved, block[group, part])
            return carry

        def displace_here(i, carry):
            row, t = own[0, 1 + i] // NB, own[0, 1 + i] % NB
            group, here = group_of(row)
            for n, part in enumerate(parts):
                moved = tops_here[pl.ds(n * NB + t, 1), :]
                block[group, part] = jnp.where(here, moved, block[group, part])
            return carry

        @pl.when(me == 0)
        def _():
            for n, part in enumerate(parts):
                tops_here[n * NB : (n + 1) * NB, :] = block[0:NB, part]

        lax.fori_loop(0, n_away, displace, 0)
        lax.fori_loop(0, n_here, displace_here, 0)
        block[:, cols] = block[:, cols] - product

        @pl.when(me == 0)
        def _():
            block[0:NB, cols] = upper

        store(k).start()
    for k in range(len(CHUNKS)):
        store(k).wait()


def update(owned, given, panels, trailing):
    rows, cols = trailing.shape
    return pl.pallas_call(
        update_kernel,
        out_shape=jax.ShapeDtypeStruct((rows, cols), F32),
        in_specs=[VMEM] * 7 + [HBM],
        out_specs=HBM,
        scratch_shapes=[
            pltpu.VMEM((rows, cols), F32),
            pltpu.VMEM((NB, cols), F32),
            pltpu.VMEM((NB, LANES), F32),
            pltpu.VMEM((4 * NB, LANES), F32),
            pltpu.VMEM((rows, 4 * NB), BF16),
            pltpu.SMEM((1, OWN), jnp.int32),
            pltpu.VMEM((NB, NB, LANES), F32),
            pltpu.SemaphoreType.DMA((len(CHUNKS),)),
            pltpu.SemaphoreType.DMA((len(CHUNKS),)),
            pltpu.SemaphoreType.DMA,
            pltpu.SemaphoreType.DMA,
        ],
        compiler_params=pltpu.CompilerParams(vmem_limit_bytes=48 * 2**20),
    )(owned, given, *panels, trailing)


def ring(step):
    return [(c, (c // 2 + step) % 4 * 2 + c % 2) for c in range(N_PCOL)]


def body(trailing, factors, pivots):
    partner = lax.ppermute(factors, "pcol", [(c, c ^ 1) for c in range(N_PCOL)])
    sent, partner = lax.optimization_barrier((pick(pivots, trailing), partner))
    pair = join(factors, partner)
    got = lax.all_to_all(sent, "prow", 0, 0)
    panels = [factors, partner] + [lax.ppermute(pair, "pcol", ring(4 - turn)) for turn in (1, 2, 3)]
    routes, owned = route(pivots)
    back = spread(routes, got.reshape(N_PROW * NB, LANES), panels)
    given = lax.all_to_all(back.reshape(N_PROW, BACK, LANES), "prow", 0, 0)
    return update(owned, given.reshape(N_PROW * BACK, LANES), panels, trailing)


def solution(mesh):
    return jax.shard_map(
        body,
        mesh=mesh,
        in_specs=(P("prow", "pcol"), P(None, ("prow", "pcol")), P()),
        out_specs=P("prow", "pcol"),
        check_vma=False,
    )
```

```python
import jax
import jax.numpy as jnp
from jax import lax
from jax.experimental import pallas as pl
from jax.experimental.pallas import tpu as pltpu
from jax.sharding import PartitionSpec as P

LANES = 128
NB = 64
N_PROW = 16
N_PCOL = 8
ROWS = 16384
LOWER = 16
BACK = NB + LOWER
F32 = jnp.float32
BF16 = jnp.bfloat16


def holder_of(row):
    return (row >> 6) & (N_PROW - 1)


def local_of(row):
    return ((row >> 10) << 6) | (row & (NB - 1))


def swap_chain(pivots, order, visit):
    for j in range(NB):
        order[pivots[j]] = pivots[j]
    for j in range(NB):
        order[j] = j
    for j in range(NB):
        k = pivots[j]
        row = order[k]
        order[k] = order[j]
        visit(j, row)


def pick_kernel(pivots, trailing, sent, order, count, rows, slots, apart, sem, top_sem):
    me = lax.axis_index("prow")

    def row_copy(row, slot, piece, target):
        return pltpu.make_async_copy(
            trailing.at[pl.ds(row, 1), pl.ds(piece * LANES, LANES)],
            target.at[piece, pl.ds(slot, 1), :],
            sem,
        )

    def top_copy(piece):
        return pltpu.make_async_copy(
            trailing.at[pl.ds(0, NB), pl.ds(piece * LANES, LANES)],
            sent.at[piece, pl.ds(0, NB), :],
            top_sem.at[piece],
        )

    @pl.when(me == 0)
    def _():
        for piece in range(N_PROW):
            top_copy(piece).start()

    count[0] = 0

    def visit(j, row):
        place = count[0]
        rows[place] = row
        slots[place] = j
        wanted = jnp.logical_and(holder_of(row) == me, row >= NB)
        count[0] = place + jnp.where(wanted, 1, 0)

    swap_chain(pivots, order, visit)
    n_mine = count[0]

    n_apart = jnp.where(me == 0, n_mine, 0)

    def send(i, carry):
        for piece in range(N_PROW):
            row_copy(local_of(rows[i]), slots[i], piece, sent).start()
        return carry

    def send_apart(i, carry):
        for piece in range(N_PROW):
            row_copy(local_of(rows[i]), i, piece, apart).start()
        return carry

    lax.fori_loop(0, n_mine - n_apart, send, 0)
    lax.fori_loop(0, n_apart, send_apart, 0)

    @pl.when(me == 0)
    def _():
        for piece in range(N_PROW):
            top_copy(piece).wait()

    def finish(i, carry):
        for piece in range(N_PROW):
            row_copy(0, 0, piece, sent).wait()
        return carry

    lax.fori_loop(0, n_mine, finish, 0)

    def replace(i, carry):
        slot = order[rows[i]]
        for piece in range(N_PROW):
            sent[piece, pl.ds(slot, 1), :] = apart[piece, pl.ds(i, 1), :]
        return carry

    lax.fori_loop(0, n_apart, replace, 0)


SMEM = pl.BlockSpec(memory_space=pltpu.SMEM)
VMEM = pl.BlockSpec(memory_space=pltpu.VMEM)
HBM = pl.BlockSpec(memory_space=pltpu.HBM)
ANY = pl.BlockSpec(memory_space=pl.ANY)


def pick(pivots, trailing):
    return pl.pallas_call(
        pick_kernel,
        out_shape=jax.ShapeDtypeStruct((N_PROW, NB, LANES), F32),
        in_specs=[SMEM, HBM],
        out_specs=VMEM,
        scratch_shapes=[
            pltpu.SMEM((ROWS,), jnp.int32),
            pltpu.SMEM((1,), jnp.int32),
            pltpu.SMEM((NB + 1,), jnp.int32),
            pltpu.SMEM((NB + 1,), jnp.int32),
            pltpu.VMEM((N_PROW, NB, LANES), F32),
            pltpu.SemaphoreType.DMA,
            pltpu.SemaphoreType.DMA((N_PROW,)),
        ],
        compiler_params=pltpu.CompilerParams(vmem_limit_bytes=58 * 2**20),
    )(pivots, trailing)


def join_kernel(mine, other, pair):
    pair[0:NB, :] = mine[...]
    pair[NB : 2 * NB, :] = other[...]


def join(mine, other):
    return pl.pallas_call(
        join_kernel,
        out_shape=jax.ShapeDtypeStruct((2 * NB, LANES), F32),
        in_specs=[VMEM, VMEM],
        out_specs=VMEM,
        compiler_params=pltpu.CompilerParams(vmem_limit_bytes=8 * 2**20),
    )(mine, other)


TARGET = NB
SOURCE = 2 * NB
ROUTES = 3 * NB
OWN = 2 * NB


def route_kernel(pivots, routes, owned, table, own, order, rows, count, sems):
    me = lax.axis_index("prow")

    def visit(j, row):
        rows[j] = row

    swap_chain(pivots, order, visit)
    count[0] = 0
    for j in range(NB):
        row = rows[j]
        holder = holder_of(row)
        outside = row >= NB
        displacer = jnp.where(outside, order[row], row)
        place = holder * NB + jnp.where(holder == 0, displacer, j)
        away = holder > 0
        table[0, j] = place
        table[0, TARGET + j] = holder * BACK + j
        table[0, SOURCE + j] = jnp.where(away, displacer, place)
        slot = count[0]
        own[0, 1 + slot] = local_of(row) * NB + jnp.where(away, j, displacer)
        count[0] = slot + jnp.where(jnp.logical_and(outside, holder == me), 1, 0)
    own[0, 0] = count[0]
    first = pltpu.make_async_copy(table, routes, sems.at[0])
    second = pltpu.make_async_copy(own, owned, sems.at[1])
    first.start()
    second.start()
    first.wait()
    second.wait()


def route(pivots):
    return pl.pallas_call(
        route_kernel,
        out_shape=(
            jax.ShapeDtypeStruct((1, ROUTES), jnp.int32),
            jax.ShapeDtypeStruct((1, OWN), jnp.int32),
        ),
        in_specs=[SMEM],
        out_specs=(VMEM, VMEM),
        scratch_shapes=[
            pltpu.SMEM((1, ROUTES), jnp.int32),
            pltpu.SMEM((1, OWN), jnp.int32),
            pltpu.SMEM((ROWS,), jnp.int32),
            pltpu.SMEM((NB,), jnp.int32),
            pltpu.SMEM((1,), jnp.int32),
            pltpu.SemaphoreType.DMA((2,)),
        ],
        compiler_params=pltpu.CompilerParams(vmem_limit_bytes=8 * 2**20),
    )(pivots)


HALF = NB // 2


def fold(diagonal):
    row_id = lax.broadcasted_iota(jnp.int32, (HALF, HALF), 0)
    col_id = lax.broadcasted_iota(jnp.int32, (HALF, HALF), 1)
    first = diagonal[0:HALF, 0:HALF]
    last = diagonal[HALF:NB, HALF:NB]
    mixed = jnp.where(col_id > row_id, first, last.T)
    both = jnp.concatenate([mixed, diagonal[0:HALF, HALF:NB]], axis=1)
    return jnp.concatenate([both[0:LOWER], both[LOWER:HALF]], axis=1)


def unfold(packed):
    row_id = lax.broadcasted_iota(jnp.int32, (HALF, HALF), 0)
    col_id = lax.broadcasted_iota(jnp.int32, (HALF, HALF), 1)
    both = jnp.concatenate([packed[:, 0:NB], packed[:, NB:LANES]], axis=0)
    mixed = both[:, 0:HALF]
    zero = jnp.zeros((HALF, HALF), F32)
    first = jnp.where(col_id < row_id, mixed.T, zero)
    last = jnp.where(col_id < row_id, mixed, zero)
    top = jnp.concatenate([first, zero], axis=1)
    return jnp.concatenate([top, jnp.concatenate([both[:, HALF:NB].T, last], axis=1)], axis=0)


def spread_kernel(routes, got, *refs):
    panels, (back, table, diagonal, sem) = refs[:5], refs[5:]
    copy = pltpu.make_async_copy(routes, table, sem)
    copy.start()
    c = lax.axis_index("pcol")
    start = pl.multiple_of(c % 2 * NB, NB)
    for side in range(2):

        @pl.when(c == side)
        def _():
            diagonal[...] = panels[side][...]

    for step, pair in enumerate(panels[2:], 1):

        @pl.when(c // 2 == 4 - step)
        def _():
            diagonal[...] = pair[pl.ds(start, NB), :]

    packed = fold(diagonal[:, 0:NB])
    for q in range(N_PROW):
        low = q * BACK + NB
        back[low : low + LOWER, :] = packed
    copy.wait()
    for j in range(NB):
        back[j : j + 1, :] = got[pl.ds(table[0, j], 1), :]
    for q in range(1, N_PROW):
        back[q * BACK : q * BACK + NB, :] = back[0:NB, :]
    for j in range(NB):
        source = got[pl.ds(table[0, SOURCE + j], 1), :]
        back[pl.ds(table[0, TARGET + j], 1), :] = source


def spread(routes, got, panels):
    return pl.pallas_call(
        spread_kernel,
        out_shape=jax.ShapeDtypeStruct((N_PROW * BACK, LANES), F32),
        in_specs=[ANY] + [VMEM] * 6,
        out_specs=VMEM,
        scratch_shapes=[
            pltpu.SMEM((1, ROUTES), jnp.int32),
            pltpu.VMEM((NB, LANES), F32),
            pltpu.SemaphoreType.DMA,
        ],
        compiler_params=pltpu.CompilerParams(vmem_limit_bytes=16 * 2**20),
    )(routes, got, *panels)


def halves(x):
    high = x.astype(BF16)
    return high, (x - high.astype(F32)).astype(BF16)


def thirds(x):
    high = x.astype(BF16)
    rest = x - high.astype(F32)
    mid = rest.astype(BF16)
    return high, mid, (rest - mid.astype(F32)).astype(BF16)


CHUNKS = ((0, 512), (512, 512), (1024, 512), (1536, 512))


def update_kernel(
    owned,
    given,
    mine,
    other,
    *refs,
):
    pairs, refs = refs[:3], refs[3:]
    trailing, updated, block, kept, chosen, tops_here, multipliers, own, columns = refs[:9]
    arrive, leave, sem, row_sem = refs[9:]
    me = lax.axis_index("prow")

    def load(k):
        cols = pl.ds(*CHUNKS[k])
        return pltpu.make_async_copy(trailing.at[:, cols], block.at[:, cols], arrive.at[k])

    def store(k):
        cols = pl.ds(*CHUNKS[k])
        return pltpu.make_async_copy(block.at[:, cols], updated.at[:, cols], leave.at[k])

    copy = pltpu.make_async_copy(owned, own, sem)
    copy.start()
    load(0).start()
    load(1).start()

    copy.wait()
    n_own = own[0, 0]
    n_away = jnp.where(me == 0, 0, n_own)
    n_here = n_own - n_away

    row_id = lax.broadcasted_iota(jnp.int32, (8, LANES), 0)

    def group_of(row):
        return pl.ds(pl.multiple_of(row // 8 * 8, 8), 8), row_id == row % 8

    def row_copy(i):
        row, j = own[0, 1 + i] // NB, own[0, 1 + i] % NB
        return pltpu.make_async_copy(
            trailing.at[pl.ds(row, 1), :], kept.at[pl.ds(j, 1), :], row_sem
        )

    def fetch(i, carry):
        row_copy(i).start()
        chosen[pl.ds(own[0, 1 + i] % NB, 1), :] = jnp.ones((1, LANES), F32)
        return carry

    def fetched(i, carry):
        row_copy(i).wait()
        return carry

    chosen[...] = jnp.zeros_like(chosen)
    lax.fori_loop(0, n_away, fetch, 0)
    for k in range(2, len(CHUNKS)):
        load(k).start()

    c = lax.axis_index("pcol")
    z, core = c // 2, c % 2

    def place(step, side, values):
        high, low = halves(values.T)
        start = (((z + step) & 3) * 2 + ((core + side) & 1)) * LANES
        rows = pl.ds(pl.multiple_of(start, LANES), LANES)
        multipliers[rows, :] = jnp.concatenate([high, low, high, low], axis=1)

    for side, panel in enumerate((mine, other)):
        place(0, side, panel[...])
        for step, pair in enumerate(pairs, 1):
            place(step, side, pair[side * NB : (side + 1) * NB, :])

    lower = unfold(given[NB:BACK, :])
    for j in range(NB):
        columns[j] = jnp.broadcast_to(lower[:, j : j + 1], (NB, LANES))

    row_id = lax.broadcasted_iota(jnp.int32, (8, LANES), 0)
    col_id = lax.broadcasted_iota(jnp.int32, (8, LANES), 1)
    inverse = [jnp.where(col_id == row_id + 8 * b, 1.0, 0.0).astype(F32) for b in range(8)]
    for j in range(NB):
        b, s = j // 8, j % 8
        row = jnp.broadcast_to(inverse[b][s : s + 1, :], (8, LANES))
        for i in range(b, 8):
            inverse[i] = inverse[i] - columns[j, 8 * i : 8 * i + 8, :] * row
    inv_high, inv_mid, inv_low = thirds(jnp.concatenate(inverse, axis=0)[:, 0:NB])
    left = jnp.concatenate([inv_high, inv_mid, inv_low, inv_high, inv_mid, inv_high], axis=1)

    lax.fori_loop(0, n_away, fetched, 0)
    for k, (start, width) in enumerate(CHUNKS):
        cols = slice(start, start + width)
        pieces = range(start // LANES, (start + width) // LANES)
        parts = [slice(p * LANES, (p + 1) * LANES) for p in pieces]
        load(k).wait()
        tops = jnp.concatenate(
            [
                jnp.where(chosen[...] > 0, kept[:, part], given[p * BACK : p * BACK + NB, :])
                for p, part in zip(pieces, parts)
            ],
            axis=1,
        )
        high, mid, low = thirds(tops)
        right = jnp.concatenate([high, high, high, mid, mid, low], axis=0)
        upper = jnp.dot(left, right, preferred_element_type=F32)
        up_high, up_low = halves(upper)
        factor = jnp.concatenate([up_high, up_high, up_low, up_low], axis=0)
        product = jnp.dot(multipliers[...], factor, preferred_element_type=F32)

        def displace(i, carry):
            row, j = own[0, 1 + i] // NB, own[0, 1 + i] % NB
            group, here = group_of(row)
            for p, part in zip(pieces, parts):
                moved = given[pl.ds(p * BACK + j, 1), :]
                block[group, part] = jnp.where(here, moved, block[group, part])
            return carry

        def displace_here(i, carry):
            row, t = own[0, 1 + i] // NB, own[0, 1 + i] % NB
            group, here = group_of(row)
            for n, part in enumerate(parts):
                moved = tops_here[pl.ds(n * NB + t, 1), :]
                block[group, part] = jnp.where(here, moved, block[group, part])
            return carry

        @pl.when(me == 0)
        def _():
            for n, part in enumerate(parts):
                tops_here[n * NB : (n + 1) * NB, :] = block[0:NB, part]

        lax.fori_loop(0, n_away, displace, 0)
        lax.fori_loop(0, n_here, displace_here, 0)
        block[:, cols] = block[:, cols] - product

        @pl.when(me == 0)
        def _():
            block[0:NB, cols] = upper

        store(k).start()
    for k in range(len(CHUNKS)):
        store(k).wait()


def update(owned, given, panels, trailing):
    rows, cols = trailing.shape
    return pl.pallas_call(
        update_kernel,
        out_shape=jax.ShapeDtypeStruct((rows, cols), F32),
        in_specs=[VMEM] * 7 + [HBM],
        out_specs=HBM,
        scratch_shapes=[
            pltpu.VMEM((rows, cols), F32),
            pltpu.VMEM((NB, cols), F32),
            pltpu.VMEM((NB, LANES), F32),
            pltpu.VMEM((4 * NB, LANES), F32),
            pltpu.VMEM((rows, 4 * NB), BF16),
            pltpu.SMEM((1, OWN), jnp.int32),
            pltpu.VMEM((NB, NB, LANES), F32),
            pltpu.SemaphoreType.DMA((len(CHUNKS),)),
            pltpu.SemaphoreType.DMA((len(CHUNKS),)),
            pltpu.SemaphoreType.DMA,
            pltpu.SemaphoreType.DMA,
        ],
        compiler_params=pltpu.CompilerParams(vmem_limit_bytes=48 * 2**20),
    )(owned, given, *panels, trailing)


def ring(step):
    return [(c, (c // 2 + step) % 4 * 2 + c % 2) for c in range(N_PCOL)]


def body(trailing, factors, pivots):
    partner = lax.ppermute(factors, "pcol", [(c, c ^ 1) for c in range(N_PCOL)])
    sent, partner = lax.optimization_barrier((pick(pivots, trailing), partner))
    pair = join(factors, partner)
    got = lax.all_to_all(sent, "prow", 0, 0)
    panels = [factors, partner] + [lax.ppermute(pair, "pcol", ring(4 - turn)) for turn in (1, 2, 3)]
    routes, owned = route(pivots)
    back = spread(routes, got.reshape(N_PROW * NB, LANES), panels)
    given = lax.all_to_all(back.reshape(N_PROW, BACK, LANES), "prow", 0, 0)
    return update(owned, given.reshape(N_PROW * BACK, LANES), panels, trailing)


def solution(mesh):
    return jax.shard_map(
        body,
        mesh=mesh,
        in_specs=(P("prow", "pcol"), P(None, ("prow", "pcol")), P()),
        out_specs=P("prow", "pcol"),
        check_vma=False,
    )
```

```python
import jax
import jax.numpy as jnp
from jax import lax
from jax.experimental import pallas as pl
from jax.experimental.pallas import tpu as pltpu
from jax.sharding import PartitionSpec as P

LANES = 128
NB = 64
N_PROW = 16
N_PCOL = 8
ROWS = 16384
LOWER = 16
BACK = NB + LOWER
F32 = jnp.float32
BF16 = jnp.bfloat16


def holder_of(row):
    return (row >> 6) & (N_PROW - 1)


def local_of(row):
    return ((row >> 10) << 6) | (row & (NB - 1))


def swap_chain(pivots, order, visit):
    for j in range(NB):
        order[pivots[j]] = pivots[j]
    for j in range(NB):
        order[j] = j
    for j in range(NB):
        k = pivots[j]
        row = order[k]
        order[k] = order[j]
        visit(j, row)


def pick_kernel(pivots, trailing, sent, order, count, rows, slots, apart, sem, top_sem):
    me = lax.axis_index("prow")

    def row_copy(row, slot, piece, target):
        return pltpu.make_async_copy(
            trailing.at[pl.ds(row, 1), pl.ds(piece * LANES, LANES)],
            target.at[piece, pl.ds(slot, 1), :],
            sem,
        )

    def top_copy(piece):
        return pltpu.make_async_copy(
            trailing.at[pl.ds(0, NB), pl.ds(piece * LANES, LANES)],
            sent.at[piece, pl.ds(0, NB), :],
            top_sem.at[piece],
        )

    @pl.when(me == 0)
    def _():
        for piece in range(N_PROW):
            top_copy(piece).start()

    count[0] = 0

    def visit(j, row):
        place = count[0]
        rows[place] = row
        slots[place] = j
        wanted = jnp.logical_and(holder_of(row) == me, row >= NB)
        count[0] = place + jnp.where(wanted, 1, 0)

    swap_chain(pivots, order, visit)
    n_mine = count[0]

    n_apart = jnp.where(me == 0, n_mine, 0)

    def send(i, carry):
        for piece in range(N_PROW):
            row_copy(local_of(rows[i]), slots[i], piece, sent).start()
        return carry

    def send_apart(i, carry):
        for piece in range(N_PROW):
            row_copy(local_of(rows[i]), i, piece, apart).start()
        return carry

    lax.fori_loop(0, n_mine - n_apart, send, 0)
    lax.fori_loop(0, n_apart, send_apart, 0)

    @pl.when(me == 0)
    def _():
        for piece in range(N_PROW):
            top_copy(piece).wait()

    def finish(i, carry):
        for piece in range(N_PROW):
            row_copy(0, 0, piece, sent).wait()
        return carry

    lax.fori_loop(0, n_mine, finish, 0)

    def replace(i, carry):
        slot = order[rows[i]]
        for piece in range(N_PROW):
            sent[piece, pl.ds(slot, 1), :] = apart[piece, pl.ds(i, 1), :]
        return carry

    lax.fori_loop(0, n_apart, replace, 0)


SMEM = pl.BlockSpec(memory_space=pltpu.SMEM)
VMEM = pl.BlockSpec(memory_space=pltpu.VMEM)
HBM = pl.BlockSpec(memory_space=pltpu.HBM)
ANY = pl.BlockSpec(memory_space=pl.ANY)


def pick(pivots, trailing):
    return pl.pallas_call(
        pick_kernel,
        out_shape=jax.ShapeDtypeStruct((N_PROW, NB, LANES), F32),
        in_specs=[SMEM, HBM],
        out_specs=VMEM,
        scratch_shapes=[
            pltpu.SMEM((ROWS,), jnp.int32),
            pltpu.SMEM((1,), jnp.int32),
            pltpu.SMEM((NB + 1,), jnp.int32),
            pltpu.SMEM((NB + 1,), jnp.int32),
            pltpu.VMEM((N_PROW, NB, LANES), F32),
            pltpu.SemaphoreType.DMA,
            pltpu.SemaphoreType.DMA((N_PROW,)),
        ],
        compiler_params=pltpu.CompilerParams(vmem_limit_bytes=58 * 2**20),
    )(pivots, trailing)


def join_kernel(mine, other, pair):
    pair[0:NB, :] = mine[...]
    pair[NB : 2 * NB, :] = other[...]


def join(mine, other):
    return pl.pallas_call(
        join_kernel,
        out_shape=jax.ShapeDtypeStruct((2 * NB, LANES), F32),
        in_specs=[VMEM, VMEM],
        out_specs=VMEM,
        compiler_params=pltpu.CompilerParams(vmem_limit_bytes=8 * 2**20),
    )(mine, other)


TARGET = NB
SOURCE = 2 * NB
ROUTES = 3 * NB
OWN = 2 * NB


def route_kernel(pivots, routes, owned, table, own, order, rows, count, sems):
    me = lax.axis_index("prow")

    def visit(j, row):
        rows[j] = row

    swap_chain(pivots, order, visit)
    count[0] = 0
    for j in range(NB):
        row = rows[j]
        holder = holder_of(row)
        outside = row >= NB
        displacer = jnp.where(outside, order[row], row)
        place = holder * NB + jnp.where(holder == 0, displacer, j)
        away = holder > 0
        table[0, j] = place
        table[0, TARGET + j] = holder * BACK + j
        table[0, SOURCE + j] = jnp.where(away, displacer, place)
        slot = count[0]
        own[0, 1 + slot] = local_of(row) * NB + jnp.where(away, j, displacer)
        count[0] = slot + jnp.where(jnp.logical_and(outside, holder == me), 1, 0)
    own[0, 0] = count[0]
    first = pltpu.make_async_copy(table, routes, sems.at[0])
    second = pltpu.make_async_copy(own, owned, sems.at[1])
    first.start()
    second.start()
    first.wait()
    second.wait()


def route(pivots):
    return pl.pallas_call(
        route_kernel,
        out_shape=(
            jax.ShapeDtypeStruct((1, ROUTES), jnp.int32),
            jax.ShapeDtypeStruct((1, OWN), jnp.int32),
        ),
        in_specs=[SMEM],
        out_specs=(VMEM, VMEM),
        scratch_shapes=[
            pltpu.SMEM((1, ROUTES), jnp.int32),
            pltpu.SMEM((1, OWN), jnp.int32),
            pltpu.SMEM((ROWS,), jnp.int32),
            pltpu.SMEM((NB,), jnp.int32),
            pltpu.SMEM((1,), jnp.int32),
            pltpu.SemaphoreType.DMA((2,)),
        ],
        compiler_params=pltpu.CompilerParams(vmem_limit_bytes=8 * 2**20),
    )(pivots)


HALF = NB // 2


def fold(diagonal):
    row_id = lax.broadcasted_iota(jnp.int32, (HALF, HALF), 0)
    col_id = lax.broadcasted_iota(jnp.int32, (HALF, HALF), 1)
    first = diagonal[0:HALF, 0:HALF]
    last = diagonal[HALF:NB, HALF:NB]
    mixed = jnp.where(col_id > row_id, first, last.T)
    both = jnp.concatenate([mixed, diagonal[0:HALF, HALF:NB]], axis=1)
    return jnp.concatenate([both[0:LOWER], both[LOWER:HALF]], axis=1)


def unfold(packed):
    row_id = lax.broadcasted_iota(jnp.int32, (HALF, HALF), 0)
    col_id = lax.broadcasted_iota(jnp.int32, (HALF, HALF), 1)
    both = jnp.concatenate([packed[:, 0:NB], packed[:, NB:LANES]], axis=0)
    mixed = both[:, 0:HALF]
    zero = jnp.zeros((HALF, HALF), F32)
    first = jnp.where(col_id < row_id, mixed.T, zero)
    last = jnp.where(col_id < row_id, mixed, zero)
    top = jnp.concatenate([first, zero], axis=1)
    return jnp.concatenate([top, jnp.concatenate([both[:, HALF:NB].T, last], axis=1)], axis=0)


def spread_kernel(routes, got, *refs):
    panels, (back, table, diagonal, sem) = refs[:5], refs[5:]
    copy = pltpu.make_async_copy(routes, table, sem)
    copy.start()
    c = lax.axis_index("pcol")
    start = pl.multiple_of(c % 2 * NB, NB)
    for side in range(2):

        @pl.when(c == side)
        def _():
            diagonal[...] = panels[side][...]

    for step, pair in enumerate(panels[2:], 1):

        @pl.when(c // 2 == 4 - step)
        def _():
            diagonal[...] = pair[pl.ds(start, NB), :]

    packed = fold(diagonal[:, 0:NB])
    for q in range(N_PROW):
        low = q * BACK + NB
        back[low : low + LOWER, :] = packed
    copy.wait()
    for j in range(NB):
        back[j : j + 1, :] = got[pl.ds(table[0, j], 1), :]
    for q in range(1, N_PROW):
        back[q * BACK : q * BACK + NB, :] = back[0:NB, :]
    for j in range(NB):
        source = got[pl.ds(table[0, SOURCE + j], 1), :]
        back[pl.ds(table[0, TARGET + j], 1), :] = source


def spread(routes, got, panels):
    return pl.pallas_call(
        spread_kernel,
        out_shape=jax.ShapeDtypeStruct((N_PROW * BACK, LANES), F32),
        in_specs=[ANY] + [VMEM] * 6,
        out_specs=VMEM,
        scratch_shapes=[
            pltpu.SMEM((1, ROUTES), jnp.int32),
            pltpu.VMEM((NB, LANES), F32),
            pltpu.SemaphoreType.DMA,
        ],
        compiler_params=pltpu.CompilerParams(vmem_limit_bytes=16 * 2**20),
    )(routes, got, *panels)


def halves(x):
    high = x.astype(BF16)
    return high, (x - high.astype(F32)).astype(BF16)


def thirds(x):
    high = x.astype(BF16)
    rest = x - high.astype(F32)
    mid = rest.astype(BF16)
    return high, mid, (rest - mid.astype(F32)).astype(BF16)


CHUNKS = ((0, 512), (512, 512), (1024, 512), (1536, 512))


def update_kernel(
    owned,
    given,
    mine,
    other,
    *refs,
):
    pairs, refs = refs[:3], refs[3:]
    trailing, updated, block, kept, chosen, tops_here, multipliers, own, columns = refs[:9]
    uppers, factors, arrive, leave, sem, row_sem = refs[9:]
    me = lax.axis_index("prow")

    def load(k):
        cols = pl.ds(*CHUNKS[k])
        return pltpu.make_async_copy(trailing.at[:, cols], block.at[:, cols], arrive.at[k])

    def store(k):
        cols = pl.ds(*CHUNKS[k])
        return pltpu.make_async_copy(block.at[:, cols], updated.at[:, cols], leave.at[k])

    copy = pltpu.make_async_copy(owned, own, sem)
    copy.start()
    load(0).start()
    load(1).start()

    copy.wait()
    n_own = own[0, 0]
    n_away = jnp.where(me == 0, 0, n_own)
    n_here = n_own - n_away

    row_id = lax.broadcasted_iota(jnp.int32, (8, LANES), 0)

    def group_of(row):
        return pl.ds(pl.multiple_of(row // 8 * 8, 8), 8), row_id == row % 8

    def row_copy(i):
        row, j = own[0, 1 + i] // NB, own[0, 1 + i] % NB
        return pltpu.make_async_copy(
            trailing.at[pl.ds(row, 1), :], kept.at[pl.ds(j, 1), :], row_sem
        )

    def fetch(i, carry):
        row_copy(i).start()
        chosen[pl.ds(own[0, 1 + i] % NB, 1), :] = jnp.ones((1, LANES), F32)
        return carry

    def fetched(i, carry):
        row_copy(i).wait()
        return carry

    chosen[...] = jnp.zeros_like(chosen)
    lax.fori_loop(0, n_away, fetch, 0)
    for k in range(2, len(CHUNKS)):
        load(k).start()

    c = lax.axis_index("pcol")
    z, core = c // 2, c % 2

    def place(step, side, values):
        high, low = halves(values.T)
        start = (((z + step) & 3) * 2 + ((core + side) & 1)) * LANES
        rows = pl.ds(pl.multiple_of(start, LANES), LANES)
        multipliers[rows, :] = jnp.concatenate([high, low, high, low], axis=1)

    for side, panel in enumerate((mine, other)):
        place(0, side, panel[...])
        for step, pair in enumerate(pairs, 1):
            place(step, side, pair[side * NB : (side + 1) * NB, :])

    lower = unfold(given[NB:BACK, :])
    for j in range(NB):
        columns[j] = jnp.broadcast_to(lower[:, j : j + 1], (NB, LANES))

    row_id = lax.broadcasted_iota(jnp.int32, (8, LANES), 0)
    col_id = lax.broadcasted_iota(jnp.int32, (8, LANES), 1)
    inverse = [jnp.where(col_id == row_id + 8 * b, 1.0, 0.0).astype(F32) for b in range(8)]
    for j in range(NB):
        b, s = j // 8, j % 8
        row = jnp.broadcast_to(inverse[b][s : s + 1, :], (8, LANES))
        for i in range(b, 8):
            inverse[i] = inverse[i] - columns[j, 8 * i : 8 * i + 8, :] * row
    inv_high, inv_mid, inv_low = thirds(jnp.concatenate(inverse, axis=0)[:, 0:NB])
    left = jnp.concatenate([inv_high, inv_mid, inv_low, inv_high, inv_mid, inv_high], axis=1)

    lax.fori_loop(0, n_away, fetched, 0)
    for start, width in CHUNKS:
        cols = slice(start, start + width)
        pieces = range(start // LANES, (start + width) // LANES)
        tops = jnp.concatenate(
            [
                jnp.where(
                    chosen[...] > 0,
                    kept[:, p * LANES : (p + 1) * LANES],
                    given[p * BACK : p * BACK + NB, :],
                )
                for p in pieces
            ],
            axis=1,
        )
        high, mid, low = thirds(tops)
        right = jnp.concatenate([high, high, high, mid, mid, low], axis=0)
        upper = jnp.dot(left, right, preferred_element_type=F32)
        uppers[:, cols] = upper
        up_high, up_low = halves(upper)
        factors[:, cols] = jnp.concatenate([up_high, up_high, up_low, up_low], axis=0)

    for k, (start, width) in enumerate(CHUNKS):
        cols = slice(start, start + width)
        pieces = range(start // LANES, (start + width) // LANES)
        parts = [slice(p * LANES, (p + 1) * LANES) for p in pieces]
        product = jnp.dot(multipliers[...], factors[:, cols], preferred_element_type=F32)
        load(k).wait()

        def displace(i, carry):
            row, j = own[0, 1 + i] // NB, own[0, 1 + i] % NB
            group, here = group_of(row)
            for p, part in zip(pieces, parts):
                moved = given[pl.ds(p * BACK + j, 1), :]
                block[group, part] = jnp.where(here, moved, block[group, part])
            return carry

        def displace_here(i, carry):
            row, t = own[0, 1 + i] // NB, own[0, 1 + i] % NB
            group, here = group_of(row)
            for n, part in enumerate(parts):
                moved = tops_here[pl.ds(n * NB + t, 1), :]
                block[group, part] = jnp.where(here, moved, block[group, part])
            return carry

        @pl.when(me == 0)
        def _():
            for n, part in enumerate(parts):
                tops_here[n * NB : (n + 1) * NB, :] = block[0:NB, part]

        lax.fori_loop(0, n_away, displace, 0)
        lax.fori_loop(0, n_here, displace_here, 0)
        block[:, cols] = block[:, cols] - product

        @pl.when(me == 0)
        def _():
            block[0:NB, cols] = uppers[:, cols]

        store(k).start()
    for k in range(len(CHUNKS)):
        store(k).wait()


def update(owned, given, panels, trailing):
    rows, cols = trailing.shape
    return pl.pallas_call(
        update_kernel,
        out_shape=jax.ShapeDtypeStruct((rows, cols), F32),
        in_specs=[VMEM] * 7 + [HBM],
        out_specs=HBM,
        scratch_shapes=[
            pltpu.VMEM((rows, cols), F32),
            pltpu.VMEM((NB, cols), F32),
            pltpu.VMEM((NB, LANES), F32),
            pltpu.VMEM((4 * NB, LANES), F32),
            pltpu.VMEM((rows, 4 * NB), BF16),
            pltpu.SMEM((1, OWN), jnp.int32),
            pltpu.VMEM((NB, NB, LANES), F32),
            pltpu.VMEM((NB, cols), F32),
            pltpu.VMEM((4 * NB, cols), BF16),
            pltpu.SemaphoreType.DMA((len(CHUNKS),)),
            pltpu.SemaphoreType.DMA((len(CHUNKS),)),
            pltpu.SemaphoreType.DMA,
            pltpu.SemaphoreType.DMA,
        ],
        compiler_params=pltpu.CompilerParams(vmem_limit_bytes=48 * 2**20),
    )(owned, given, *panels, trailing)


def ring(step):
    return [(c, (c // 2 + step) % 4 * 2 + c % 2) for c in range(N_PCOL)]


def body(trailing, factors, pivots):
    partner = lax.ppermute(factors, "pcol", [(c, c ^ 1) for c in range(N_PCOL)])
    sent, partner = lax.optimization_barrier((pick(pivots, trailing), partner))
    pair = join(factors, partner)
    got = lax.all_to_all(sent, "prow", 0, 0)
    panels = [factors, partner] + [lax.ppermute(pair, "pcol", ring(4 - turn)) for turn in (1, 2, 3)]
    routes, owned = route(pivots)
    back = spread(routes, got.reshape(N_PROW * NB, LANES), panels)
    given = lax.all_to_all(back.reshape(N_PROW, BACK, LANES), "prow", 0, 0)
    return update(owned, given.reshape(N_PROW * BACK, LANES), panels, trailing)


def solution(mesh):
    return jax.shard_map(
        body,
        mesh=mesh,
        in_specs=(P("prow", "pcol"), P(None, ("prow", "pcol")), P()),
        out_specs=P("prow", "pcol"),
        check_vma=False,
    )
```

```python
import jax
import jax.numpy as jnp
from jax import lax
from jax.experimental import pallas as pl
from jax.experimental.pallas import tpu as pltpu
from jax.sharding import PartitionSpec as P

LANES = 128
NB = 64
N_PROW = 16
N_PCOL = 8
ROWS = 16384
LOWER = 16
BACK = NB + LOWER
F32 = jnp.float32
BF16 = jnp.bfloat16


def holder_of(row):
    return (row >> 6) & (N_PROW - 1)


def local_of(row):
    return ((row >> 10) << 6) | (row & (NB - 1))


def swap_chain(pivots, order, visit):
    for j in range(NB):
        order[pivots[j]] = pivots[j]
    for j in range(NB):
        order[j] = j
    for j in range(NB):
        k = pivots[j]
        row = order[k]
        order[k] = order[j]
        visit(j, row)


def pick_kernel(pivots, trailing, sent, order, count, rows, slots, apart, sem, top_sem):
    me = lax.axis_index("prow")

    def row_copy(row, slot, piece, target):
        return pltpu.make_async_copy(
            trailing.at[pl.ds(row, 1), pl.ds(piece * LANES, LANES)],
            target.at[piece, pl.ds(slot, 1), :],
            sem,
        )

    def top_copy(piece):
        return pltpu.make_async_copy(
            trailing.at[pl.ds(0, NB), pl.ds(piece * LANES, LANES)],
            sent.at[piece, pl.ds(0, NB), :],
            top_sem.at[piece],
        )

    @pl.when(me == 0)
    def _():
        for piece in range(N_PROW):
            top_copy(piece).start()

    count[0] = 0

    def visit(j, row):
        place = count[0]
        rows[place] = row
        slots[place] = j
        wanted = jnp.logical_and(holder_of(row) == me, row >= NB)
        count[0] = place + jnp.where(wanted, 1, 0)

    swap_chain(pivots, order, visit)
    n_mine = count[0]

    n_apart = jnp.where(me == 0, n_mine, 0)

    def send(i, carry):
        for piece in range(N_PROW):
            row_copy(local_of(rows[i]), slots[i], piece, sent).start()
        return carry

    def send_apart(i, carry):
        for piece in range(N_PROW):
            row_copy(local_of(rows[i]), i, piece, apart).start()
        return carry

    lax.fori_loop(0, n_mine - n_apart, send, 0)
    lax.fori_loop(0, n_apart, send_apart, 0)

    @pl.when(me == 0)
    def _():
        for piece in range(N_PROW):
            top_copy(piece).wait()

    def finish(i, carry):
        for piece in range(N_PROW):
            row_copy(0, 0, piece, sent).wait()
        return carry

    lax.fori_loop(0, n_mine, finish, 0)

    def replace(i, carry):
        slot = order[rows[i]]
        for piece in range(N_PROW):
            sent[piece, pl.ds(slot, 1), :] = apart[piece, pl.ds(i, 1), :]
        return carry

    lax.fori_loop(0, n_apart, replace, 0)


SMEM = pl.BlockSpec(memory_space=pltpu.SMEM)
VMEM = pl.BlockSpec(memory_space=pltpu.VMEM)
HBM = pl.BlockSpec(memory_space=pltpu.HBM)
ANY = pl.BlockSpec(memory_space=pl.ANY)


def pick(pivots, trailing):
    return pl.pallas_call(
        pick_kernel,
        out_shape=jax.ShapeDtypeStruct((N_PROW, NB, LANES), F32),
        in_specs=[SMEM, HBM],
        out_specs=VMEM,
        scratch_shapes=[
            pltpu.SMEM((ROWS,), jnp.int32),
            pltpu.SMEM((1,), jnp.int32),
            pltpu.SMEM((NB + 1,), jnp.int32),
            pltpu.SMEM((NB + 1,), jnp.int32),
            pltpu.VMEM((N_PROW, NB, LANES), F32),
            pltpu.SemaphoreType.DMA,
            pltpu.SemaphoreType.DMA((N_PROW,)),
        ],
        compiler_params=pltpu.CompilerParams(vmem_limit_bytes=58 * 2**20),
    )(pivots, trailing)


def join_kernel(mine, other, pair):
    pair[0:NB, :] = mine[...]
    pair[NB : 2 * NB, :] = other[...]


def join(mine, other):
    return pl.pallas_call(
        join_kernel,
        out_shape=jax.ShapeDtypeStruct((2 * NB, LANES), F32),
        in_specs=[VMEM, VMEM],
        out_specs=VMEM,
        compiler_params=pltpu.CompilerParams(vmem_limit_bytes=8 * 2**20),
    )(mine, other)


TARGET = NB
SOURCE = 2 * NB
ROUTES = 3 * NB
OWN = 2 * NB


def route_kernel(pivots, routes, owned, table, own, order, rows, count, sems):
    me = lax.axis_index("prow")

    def visit(j, row):
        rows[j] = row

    swap_chain(pivots, order, visit)
    count[0] = 0
    for j in range(NB):
        row = rows[j]
        holder = holder_of(row)
        outside = row >= NB
        displacer = jnp.where(outside, order[row], row)
        place = holder * NB + jnp.where(holder == 0, displacer, j)
        away = holder > 0
        table[0, j] = place
        table[0, TARGET + j] = holder * BACK + j
        table[0, SOURCE + j] = jnp.where(away, displacer, place)
        slot = count[0]
        own[0, 1 + slot] = local_of(row) * NB + jnp.where(away, j, displacer)
        count[0] = slot + jnp.where(jnp.logical_and(outside, holder == me), 1, 0)
    own[0, 0] = count[0]
    first = pltpu.make_async_copy(table, routes, sems.at[0])
    second = pltpu.make_async_copy(own, owned, sems.at[1])
    first.start()
    second.start()
    first.wait()
    second.wait()


def route(pivots):
    return pl.pallas_call(
        route_kernel,
        out_shape=(
            jax.ShapeDtypeStruct((1, ROUTES), jnp.int32),
            jax.ShapeDtypeStruct((1, OWN), jnp.int32),
        ),
        in_specs=[SMEM],
        out_specs=(VMEM, VMEM),
        scratch_shapes=[
            pltpu.SMEM((1, ROUTES), jnp.int32),
            pltpu.SMEM((1, OWN), jnp.int32),
            pltpu.SMEM((ROWS,), jnp.int32),
            pltpu.SMEM((NB,), jnp.int32),
            pltpu.SMEM((1,), jnp.int32),
            pltpu.SemaphoreType.DMA((2,)),
        ],
        compiler_params=pltpu.CompilerParams(vmem_limit_bytes=8 * 2**20),
    )(pivots)


HALF = NB // 2


def fold(diagonal):
    row_id = lax.broadcasted_iota(jnp.int32, (HALF, HALF), 0)
    col_id = lax.broadcasted_iota(jnp.int32, (HALF, HALF), 1)
    first = diagonal[0:HALF, 0:HALF]
    last = diagonal[HALF:NB, HALF:NB]
    mixed = jnp.where(col_id > row_id, first, last.T)
    both = jnp.concatenate([mixed, diagonal[0:HALF, HALF:NB]], axis=1)
    return jnp.concatenate([both[0:LOWER], both[LOWER:HALF]], axis=1)


def unfold(packed):
    row_id = lax.broadcasted_iota(jnp.int32, (HALF, HALF), 0)
    col_id = lax.broadcasted_iota(jnp.int32, (HALF, HALF), 1)
    both = jnp.concatenate([packed[:, 0:NB], packed[:, NB:LANES]], axis=0)
    mixed = both[:, 0:HALF]
    zero = jnp.zeros((HALF, HALF), F32)
    first = jnp.where(col_id < row_id, mixed.T, zero)
    last = jnp.where(col_id < row_id, mixed, zero)
    top = jnp.concatenate([first, zero], axis=1)
    return jnp.concatenate([top, jnp.concatenate([both[:, HALF:NB].T, last], axis=1)], axis=0)


def spread_kernel(routes, got, *refs):
    panels, (back, table, diagonal, sem) = refs[:5], refs[5:]
    copy = pltpu.make_async_copy(routes, table, sem)
    copy.start()
    c = lax.axis_index("pcol")
    start = pl.multiple_of(c % 2 * NB, NB)
    for side in range(2):

        @pl.when(c == side)
        def _():
            diagonal[...] = panels[side][...]

    for step, pair in enumerate(panels[2:], 1):

        @pl.when(c // 2 == 4 - step)
        def _():
            diagonal[...] = pair[pl.ds(start, NB), :]

    packed = fold(diagonal[:, 0:NB])
    for q in range(N_PROW):
        low = q * BACK + NB
        back[low : low + LOWER, :] = packed
    copy.wait()
    for j in range(NB):
        back[j : j + 1, :] = got[pl.ds(table[0, j], 1), :]
    for q in range(1, N_PROW):
        back[q * BACK : q * BACK + NB, :] = back[0:NB, :]
    for j in range(NB):
        source = got[pl.ds(table[0, SOURCE + j], 1), :]
        back[pl.ds(table[0, TARGET + j], 1), :] = source


def spread(routes, got, panels):
    return pl.pallas_call(
        spread_kernel,
        out_shape=jax.ShapeDtypeStruct((N_PROW * BACK, LANES), F32),
        in_specs=[ANY] + [VMEM] * 6,
        out_specs=VMEM,
        scratch_shapes=[
            pltpu.SMEM((1, ROUTES), jnp.int32),
            pltpu.VMEM((NB, LANES), F32),
            pltpu.SemaphoreType.DMA,
        ],
        compiler_params=pltpu.CompilerParams(vmem_limit_bytes=16 * 2**20),
    )(routes, got, *panels)


def halves(x):
    high = x.astype(BF16)
    return high, (x - high.astype(F32)).astype(BF16)


def thirds(x):
    high = x.astype(BF16)
    rest = x - high.astype(F32)
    mid = rest.astype(BF16)
    return high, mid, (rest - mid.astype(F32)).astype(BF16)


CHUNKS = ((0, 512), (512, 512), (1024, 512), (1536, 512))


def update_kernel(
    owned,
    given,
    mine,
    other,
    *refs,
):
    pairs, refs = refs[:3], refs[3:]
    trailing, updated, block, kept, chosen, tops_here, multipliers, own, columns = refs[:9]
    uppers, factors, arrive, leave, sem, row_sem = refs[9:]
    me = lax.axis_index("prow")

    def load(k):
        cols = pl.ds(*CHUNKS[k])
        return pltpu.make_async_copy(trailing.at[:, cols], block.at[:, cols], arrive.at[k])

    def store(k):
        cols = pl.ds(*CHUNKS[k])
        return pltpu.make_async_copy(block.at[:, cols], updated.at[:, cols], leave.at[k])

    copy = pltpu.make_async_copy(owned, own, sem)
    copy.start()
    load(0).start()

    copy.wait()
    n_own = own[0, 0]
    n_away = jnp.where(me == 0, 0, n_own)
    n_here = n_own - n_away

    row_id = lax.broadcasted_iota(jnp.int32, (8, LANES), 0)

    def group_of(row):
        return pl.ds(pl.multiple_of(row // 8 * 8, 8), 8), row_id == row % 8

    def row_copy(i):
        row, j = own[0, 1 + i] // NB, own[0, 1 + i] % NB
        return pltpu.make_async_copy(
            trailing.at[pl.ds(row, 1), :], kept.at[pl.ds(j, 1), :], row_sem
        )

    def fetch(i, carry):
        row_copy(i).start()
        chosen[pl.ds(own[0, 1 + i] % NB, 1), :] = jnp.ones((1, LANES), F32)
        return carry

    def fetched(i, carry):
        row_copy(i).wait()
        return carry

    chosen[...] = jnp.zeros_like(chosen)
    lax.fori_loop(0, n_away, fetch, 0)
    for k in range(1, len(CHUNKS)):
        load(k).start()

    c = lax.axis_index("pcol")
    z, core = c // 2, c % 2

    def place(step, side, values):
        high, low = halves(values.T)
        start = (((z + step) & 3) * 2 + ((core + side) & 1)) * LANES
        rows = pl.ds(pl.multiple_of(start, LANES), LANES)
        multipliers[rows, :] = jnp.concatenate([high, low, high, low], axis=1)

    for side, panel in enumerate((mine, other)):
        place(0, side, panel[...])
        for step, pair in enumerate(pairs, 1):
            place(step, side, pair[side * NB : (side + 1) * NB, :])

    lower = unfold(given[NB:BACK, :])
    for j in range(NB):
        columns[j] = jnp.broadcast_to(lower[:, j : j + 1], (NB, LANES))

    row_id = lax.broadcasted_iota(jnp.int32, (8, LANES), 0)
    col_id = lax.broadcasted_iota(jnp.int32, (8, LANES), 1)
    inverse = [jnp.where(col_id == row_id + 8 * b, 1.0, 0.0).astype(F32) for b in range(8)]
    for j in range(NB):
        b, s = j // 8, j % 8
        row = jnp.broadcast_to(inverse[b][s : s + 1, :], (8, LANES))
        for i in range(b, 8):
            inverse[i] = inverse[i] - columns[j, 8 * i : 8 * i + 8, :] * row
    inv_high, inv_mid, inv_low = thirds(jnp.concatenate(inverse, axis=0)[:, 0:NB])
    left = jnp.concatenate([inv_high, inv_mid, inv_low, inv_high, inv_mid, inv_high], axis=1)

    lax.fori_loop(0, n_away, fetched, 0)
    for start, width in CHUNKS:
        cols = slice(start, start + width)
        pieces = range(start // LANES, (start + width) // LANES)
        tops = jnp.concatenate(
            [
                jnp.where(
                    chosen[...] > 0,
                    kept[:, p * LANES : (p + 1) * LANES],
                    given[p * BACK : p * BACK + NB, :],
                )
                for p in pieces
            ],
            axis=1,
        )
        high, mid, low = thirds(tops)
        right = jnp.concatenate([high, high, high, mid, mid, low], axis=0)
        upper = jnp.dot(left, right, preferred_element_type=F32)
        uppers[:, cols] = upper
        up_high, up_low = halves(upper)
        factors[:, cols] = jnp.concatenate([up_high, up_high, up_low, up_low], axis=0)

    for k, (start, width) in enumerate(CHUNKS):
        cols = slice(start, start + width)
        pieces = range(start // LANES, (start + width) // LANES)
        parts = [slice(p * LANES, (p + 1) * LANES) for p in pieces]
        product = jnp.dot(multipliers[...], factors[:, cols], preferred_element_type=F32)
        load(k).wait()

        def displace(i, carry):
            row, j = own[0, 1 + i] // NB, own[0, 1 + i] % NB
            group, here = group_of(row)
            for p, part in zip(pieces, parts):
                moved = given[pl.ds(p * BACK + j, 1), :]
                block[group, part] = jnp.where(here, moved, block[group, part])
            return carry

        def displace_here(i, carry):
            row, t = own[0, 1 + i] // NB, own[0, 1 + i] % NB
            group, here = group_of(row)
            for n, part in enumerate(parts):
                moved = tops_here[pl.ds(n * NB + t, 1), :]
                block[group, part] = jnp.where(here, moved, block[group, part])
            return carry

        @pl.when(me == 0)
        def _():
            for n, part in enumerate(parts):
                tops_here[n * NB : (n + 1) * NB, :] = block[0:NB, part]

        lax.fori_loop(0, n_away, displace, 0)
        lax.fori_loop(0, n_here, displace_here, 0)
        block[:, cols] = block[:, cols] - product

        @pl.when(me == 0)
        def _():
            block[0:NB, cols] = uppers[:, cols]

        store(k).start()
    for k in range(len(CHUNKS)):
        store(k).wait()


def update(owned, given, panels, trailing):
    rows, cols = trailing.shape
    return pl.pallas_call(
        update_kernel,
        out_shape=jax.ShapeDtypeStruct((rows, cols), F32),
        in_specs=[VMEM] * 7 + [HBM],
        out_specs=HBM,
        scratch_shapes=[
            pltpu.VMEM((rows, cols), F32),
            pltpu.VMEM((NB, cols), F32),
            pltpu.VMEM((NB, LANES), F32),
            pltpu.VMEM((4 * NB, LANES), F32),
            pltpu.VMEM((rows, 4 * NB), BF16),
            pltpu.SMEM((1, OWN), jnp.int32),
            pltpu.VMEM((NB, NB, LANES), F32),
            pltpu.VMEM((NB, cols), F32),
            pltpu.VMEM((4 * NB, cols), BF16),
            pltpu.SemaphoreType.DMA((len(CHUNKS),)),
            pltpu.SemaphoreType.DMA((len(CHUNKS),)),
            pltpu.SemaphoreType.DMA,
            pltpu.SemaphoreType.DMA,
        ],
        compiler_params=pltpu.CompilerParams(vmem_limit_bytes=48 * 2**20),
    )(owned, given, *panels, trailing)


def ring(step):
    return [(c, (c // 2 + step) % 4 * 2 + c % 2) for c in range(N_PCOL)]


def body(trailing, factors, pivots):
    partner = lax.ppermute(factors, "pcol", [(c, c ^ 1) for c in range(N_PCOL)])
    sent, partner = lax.optimization_barrier((pick(pivots, trailing), partner))
    pair = join(factors, partner)
    got = lax.all_to_all(sent, "prow", 0, 0)
    panels = [factors, partner] + [lax.ppermute(pair, "pcol", ring(4 - turn)) for turn in (1, 2, 3)]
    routes, owned = route(pivots)
    back = spread(routes, got.reshape(N_PROW * NB, LANES), panels)
    given = lax.all_to_all(back.reshape(N_PROW, BACK, LANES), "prow", 0, 0)
    return update(owned, given.reshape(N_PROW * BACK, LANES), panels, trailing)


def solution(mesh):
    return jax.shard_map(
        body,
        mesh=mesh,
        in_specs=(P("prow", "pcol"), P(None, ("prow", "pcol")), P()),
        out_specs=P("prow", "pcol"),
        check_vma=False,
    )
```
